256 devices in a mesh: gx: 32 (over y, z), gy: 8 (over x, core).
Axes of the slice: x: 4, y: 4, z: 8, core: 2. Of those that a mesh axis runs over, the one named last changes fastest.
Arguments:
- dual_ops: bfloat16 [128, 32, 512, 512], P('gx', 'gy'), may hold values from -2 to 8, as said below
- dual_load: float32 [128, 32, 2, 128], P('gx', 'gy'), may hold values from -100 to 100
- mode_images: float32 [128, 32, 3, 512], P('gx', 'gy'), may hold values from -0.25 to 0.25
- mode_loads: float32 [128, 32, 3], P('gx', 'gy'), may hold values from -24 to 24
- coarse_factor: float32 [12288, 12288], P(('gx', 'gy')), may hold values from -1 to 2
- west_map: int32 [128, 32, 128], P('gx', 'gy'), may hold values from 0 to 127, each once within a row
- south_map: int32 [128, 32, 128], P('gx', 'gy'), may hold values from 0 to 127, each once within a row
- mode_owner: int32 [12288], P(('gx', 'gy')), may hold values from 0 to 47, as said below
Outputs:
- multipliers: float32 [128, 32, 2, 128], P('gx', 'gy')
- projected_gradient: float32 [128, 32, 2, 128], P('gx', 'gy')
- amplitudes: float32 [128, 32, 3], P('gx', 'gy')
The draws below stay inside these ranges and needn't reach their ends.
Inputs may be any that keep to these rules, and one draw needn't show every extreme that they name: west_map[x, y] is a permutation: entry j is the index, within the east side of subdomain (x - 1, y), of the multiplier at position j of the west side of subdomain (x, y). south_map[x, y] is a permutation: entry j is the index, within the north side of subdomain (x, y - 1), of the multiplier at position j of the south side of subdomain (x, y). `mode_owner`: each aligned block of 48 entries is a permutation. dual_ops(x, y) is symmetric.
All inputs are finite; a program needn't handle non-finite values.
Results may differ from the reference program's by a relative error of at most 0.0011.
Values sent between devices are 32-bit elements; how exact they have to be, the bound alone decides.
No kernel may reach another device: no remote copies, remote signals or barrier semaphores. Data moves between devices by JAX's collectives and lax.ppermute only.
A program may use at most 64 MiB of HBM per device.

```python
import math
import jax
import jax.numpy as jnp
from jax import lax

E = 128
M = 512
MODES = 3
BX = 4
BY = 4
ITERS = 2
SX = 128
SY = 32
K = 48
NC = 12288


def draw_dual_ops(key, part):
    first, second = jax.random.split(jax.random.fold_in(key, 11))
    shape = (SX, SY, M, M)
    noise = jax.random.normal(first, shape, jnp.float32)
    diagonal = jax.random.uniform(second, (SX, SY, M, 1), jnp.float32, 3.0, 6.0)
    coupled = (noise + jnp.swapaxes(noise, 2, 3)) * (0.8 / math.sqrt(M))
    same = lax.broadcasted_iota(jnp.int32, (M, M), 0) == lax.broadcasted_iota(jnp.int32, (M, M), 1)
    return (coupled + jnp.where(same, 1.0, 0.0) * diagonal).astype(jnp.bfloat16)


def draw_dual_load(key, part):
    shape = (SX, SY, 2, E)
    column = lax.broadcasted_iota(jnp.int32, shape, 0).astype(jnp.float32)
    row_place = lax.broadcasted_iota(jnp.int32, shape, 1).astype(jnp.float32)
    level = 0.5 * (column + 0.5) / SX + 0.5 * (row_place + 0.5) / SY
    noise = jax.random.normal(key, shape, jnp.float32)
    return noise * jnp.exp(2.302585 * level)


def draw_coarse_factor(key, part):
    first, second = jax.random.split(jax.random.fold_in(key, 23))
    row_index = lax.broadcasted_iota(jnp.int32, (NC, NC), 0)
    col_index = lax.broadcasted_iota(jnp.int32, (NC, NC), 1)
    spread = jax.random.normal(first, (NC, NC), jnp.float32)
    diagonal = jax.random.uniform(second, (NC, 1), jnp.float32, 0.6, 1.4)
    scaled = spread * (0.8 / math.sqrt(NC))
    return jnp.where(row_index > col_index, scaled, 0.0) + jnp.where(row_index == col_index, 1.0, 0.0) * diagonal


def draw_mode_owner(key, part):
    shape = (NC // K, K)
    scores = jax.random.randint(key, shape, 0, 1 << 20) * K + lax.broadcasted_iota(jnp.int32, shape, 1)
    return jnp.argsort(scores, axis=1).astype(jnp.int32).reshape(NC)


def level_of(rng, shape, cuts, least, largest):
    gain = 1.0
    for position, blocks in cuts:
        heights = jax.random.uniform(jax.random.fold_in(jax.random.fold_in(rng, 6), position), (blocks,), jnp.float32, least / len(cuts), largest / len(cuts))
        gain = gain * jnp.repeat(jnp.exp(heights), shape[position] // blocks).reshape((-1,) + (1,) * (len(shape) - 1 - position))
    return gain


def bell_draw(own_key, shape, scale, reach, cuts=(), dtype=jnp.bfloat16):
    level = level_of(own_key, shape, cuts, -0.22, 0.18) if cuts else 1.0
    entries = jax.random.normal(own_key, shape, jnp.float32) * scale * level
    return jnp.minimum(jnp.maximum(entries, -reach), reach).astype(dtype)


def setup_inputs(seed: int = 0) -> dict:
    arg_keys = jax.random.split(jax.random.key(seed), 9)
    dual_ops = draw_dual_ops(jax.random.fold_in(arg_keys[8], 71), 0)
    dual_load = draw_dual_load(jax.random.fold_in(arg_keys[8], 71), 0)
    mode_images = bell_draw(arg_keys[2], (SX, SY, MODES, M), M ** -0.5, 0.25, ((0, 32), (1, 8)), jnp.float32)
    mode_loads = bell_draw(arg_keys[3], (SX, SY, MODES), 4.0, 24.0, ((0, 32), (1, 8)), jnp.float32)
    coarse_factor = draw_coarse_factor(jax.random.fold_in(arg_keys[8], 71), 0)
    west_map = jax.vmap(lambda own: jax.random.permutation(own, E))(jax.random.split(arg_keys[5], SX * SY)).reshape((SX, SY, E)).astype(jnp.int32)
    south_map = jax.vmap(lambda own: jax.random.permutation(own, E))(jax.random.split(arg_keys[6], SX * SY)).reshape((SX, SY, E)).astype(jnp.int32)
    mode_owner = draw_mode_owner(jax.random.fold_in(arg_keys[8], 71), 0)
    return dict(dual_ops=dual_ops, dual_load=dual_load, mode_images=mode_images, mode_loads=mode_loads, coarse_factor=coarse_factor, west_map=west_map, south_map=south_map, mode_owner=mode_owner)


EXACT = lax.Precision.HIGHEST


def interface(value, west_map, south_map, west_back, south_back):
    edge_size = value.shape[-1] // 4
    west = value[..., 0:edge_size]
    east = value[..., edge_size:2 * edge_size]
    south = value[..., 2 * edge_size:3 * edge_size]
    north = value[..., 3 * edge_size:]
    moved_west = jnp.take_along_axis(west, west_back, axis=-1)
    moved_south = jnp.take_along_axis(south, south_back, axis=-1)
    east_edge = east - jnp.concatenate([moved_west[1:], jnp.zeros_like(moved_west[:1])], axis=0)
    north_edge = north - jnp.concatenate([moved_south[:, 1:], jnp.zeros_like(moved_south[:, :1])], axis=1)
    west_edge = jnp.concatenate([jnp.zeros_like(east_edge[:1]), east_edge[:-1]], axis=0)
    south_edge = jnp.concatenate([jnp.zeros_like(north_edge[:, :1]), north_edge[:, :-1]], axis=1)
    west_side = -jnp.take_along_axis(west_edge, west_map, axis=-1)
    south_side = -jnp.take_along_axis(south_edge, south_map, axis=-1)
    return jnp.concatenate([west_side, east_edge, south_side, north_edge], axis=-1)


def owned(left, right):
    edge_size = left.shape[-1] // 4
    first = jnp.sum(left[..., edge_size:2 * edge_size] * right[..., edge_size:2 * edge_size])
    return first + jnp.sum(left[..., 3 * edge_size:] * right[..., 3 * edge_size:])


def owned_sides(local):
    edge_size = local.shape[-1] // 4
    return jnp.stack([local[..., edge_size:2 * edge_size], local[..., 3 * edge_size:]], axis=2)


def flatten(coarse, owner_blocks):
    block_cols = SX // BX
    block_rows = SY // BY
    grid = coarse.reshape(block_cols, BX, block_rows, BY, MODES).transpose(0, 2, 1, 3, 4)
    grid = grid.reshape(block_cols * block_rows, K)
    return jnp.take_along_axis(grid, owner_blocks, axis=1).reshape(NC)


def unflatten(vector, owner_back):
    block_cols = SX // BX
    block_rows = SY // BY
    grid = jnp.take_along_axis(vector.reshape(block_cols * block_rows, K), owner_back, axis=1)
    grid = grid.reshape(block_cols, block_rows, BX, BY, MODES).transpose(0, 2, 1, 3, 4)
    return grid.reshape(SX, SY, MODES)


def coarse_apply(coarse_factor, vector):
    inner_vec = jnp.dot(coarse_factor, vector, precision=EXACT, preferred_element_type=jnp.float32)
    return jnp.dot(inner_vec, coarse_factor, precision=EXACT, preferred_element_type=jnp.float32)


def apply_products(dual_ops, local):
    rounded = local.astype(jnp.bfloat16)

    def column(pair):
        return jnp.einsum("ymn,yn->ym", pair[0].astype(jnp.float32), pair[1].astype(jnp.float32))

    return lax.map(column, (dual_ops, rounded))


def reference(dual_ops, dual_load, mode_images, mode_loads, coarse_factor, west_map, south_map, mode_owner):
    west_back = jnp.argsort(west_map, axis=-1).astype(jnp.int32)
    south_back = jnp.argsort(south_map, axis=-1).astype(jnp.int32)
    owner_blocks = mode_owner.reshape(NC // K, K)
    owner_back = jnp.argsort(owner_blocks, axis=1).astype(jnp.int32)

    def cross(value):
        return interface(value, west_map, south_map, west_back, south_back)

    def solve(coarse):
        return unflatten(coarse_apply(coarse_factor, flatten(coarse, owner_blocks)), owner_back)

    def project(local):
        return solve(jnp.einsum("xyrm,xym->xyr", mode_images, local, precision=EXACT))

    def lift(amounts):
        return cross(jnp.einsum("xyrm,xyr->xym", mode_images, amounts, precision=EXACT))

    def apply_dual(local):
        return cross(apply_products(dual_ops, local))

    zeros_edge = jnp.zeros_like(dual_load[:, :, 0])
    target = cross(jnp.concatenate([zeros_edge, dual_load[:, :, 0], zeros_edge, dual_load[:, :, 1]], axis=-1))
    multipliers = lift(solve(mode_loads))
    residual = target - apply_dual(multipliers)
    amplitudes = project(residual)
    gradient = residual - lift(amplitudes)
    direction = gradient
    norm_now = owned(gradient, gradient)
    for iteration in range(ITERS):
        image = apply_dual(direction)
        alpha = norm_now / owned(direction, image)
        multipliers = multipliers + alpha * direction
        residual = residual - alpha * image
        amplitudes = project(residual)
        gradient = residual - lift(amplitudes)
        norm_next = owned(gradient, gradient)
        direction = gradient + (norm_next / norm_now) * direction
        norm_now = norm_next
    return owned_sides(multipliers), owned_sides(gradient), -amplitudes
```

```python
import jax
import jax.numpy as jnp
from jax import lax
from jax.experimental import pallas as pl
from jax.experimental.pallas import tpu as pltpu
from jax.sharding import PartitionSpec as P

GX, GY = "gx", "gy"
ALL = (GX, GY)
SUB = 16
E = 128
MODES = 3
BLOCK = 48
PEERS = 256
LANES = 128

AT_W, AT_E, AT_S, AT_N, AT_SCALAR = 48, 60, 72, 84, 96


def lane_gather(values, index):
    return jnp.take_along_axis(values, index, axis=1)


def up(values, rows):
    return pltpu.roll(values, values.shape[0] - rows, 0)


def down(values, rows):
    return pltpu.roll(values, rows, 0)


class Local:
    def __init__(self, refs):
        self.refs = refs
        s = lax.broadcasted_iota(jnp.int32, (SUB, LANES), 0)
        self.lane = lax.broadcasted_iota(jnp.int32, (SUB, LANES), 1)
        x = lax.shift_right_logical(s, 2)
        y = lax.bitwise_and(s, 3)
        self.x, self.y, self.s = x, y, s

    def own_at(self, r):
        return 3 * self.s + r

    def west_at(self, r):
        return AT_W + 3 * self.y + r

    def east_at(self, r):
        return AT_E + 3 * self.y + r

    def south_at(self, r):
        return AT_S + 3 * self.x + r

    def north_at(self, r):
        return AT_N + 3 * self.x + r

    def cross(self, w, t, nb):
        x, y = self.x, self.y
        nb_tw, nb_we, nb_ts, nb_wn = nb
        keep_w, keep_s, wmap, smap = (self.refs[k][...] for k in ("kw", "ks", "wmap", "smap"))
        east = w[1] - up(jnp.where(x == 0, nb_tw, t[0]), 4)
        north = w[3] - jnp.where(y == 3, down(nb_ts, 3), up(t[1], 1))
        from_west = down(jnp.where(x == 3, nb_we, w[1]), 4)
        from_south = jnp.where(y == 0, up(nb_wn, 3), down(w[3], 1))
        west = keep_w * (w[0] - lane_gather(from_west, wmap))
        south = keep_s * (w[2] - lane_gather(from_south, smap))
        return west, east, south, north

    def modes(self, r, side):
        return self.refs["m"][r, :, side * E : (side + 1) * E]

    def lift(self, row):
        a = jnp.broadcast_to(row, (SUB, LANES))
        refs = self.refs
        w = [0.0] * 4
        t = [0.0] * 2
        nb = [0.0] * 4
        for r in range(MODES):
            own = lane_gather(a, self.own_at(r))
            for side in range(4):
                w[side] += self.modes(r, side) * own
            t[0] += refs["tmw"][r] * own
            t[1] += refs["tms"][r] * own
            nb[0] += refs["nb_tmw"][r] * lane_gather(a, self.east_at(r))
            nb[1] += refs["nb_me"][r] * lane_gather(a, self.west_at(r))
            nb[2] += refs["nb_tms"][r] * lane_gather(a, self.north_at(r))
            nb[3] += refs["nb_mn"][r] * lane_gather(a, self.south_at(r))
        return self.cross(w, t, nb)

    def put(self, total, values, at, rows=None):
        here = self.lane == at
        if rows is not None:
            here = here & rows
        return total + jnp.where(here, jnp.sum(values, axis=1, keepdims=True), 0.0)

    def absorb(self, total, u):
        for r in range(MODES):
            terms = sum(self.modes(r, side) * u[side] for side in range(4))
            total = self.put(total, terms, self.own_at(r))
        return total

    def contributions(self, w, t):
        refs, x, y = self.refs, self.x, self.y
        none = jnp.zeros((SUB, LANES), jnp.float32)
        total = self.absorb(none, self.cross(w, t, (none, none, none, none)))
        to_e, to_w = down(w[1], 4), up(t[0], 4)
        to_n, to_s = up(w[3], 3), down(t[1], 3)
        for r in range(MODES):
            total = self.put(total, -refs["nb_tmw"][r] * to_e, self.east_at(r), x == 0)
            total = self.put(total, -refs["nb_me"][r] * to_w, self.west_at(r), x == 3)
            total = self.put(total, -refs["nb_tms"][r] * to_n, self.north_at(r), y == 0)
            total = self.put(total, -refs["nb_mn"][r] * to_s, self.south_at(r), y == 3)
        return total

    def dual(self, u, precise):
        ops = self.refs["ops"]
        whole = jnp.concatenate(u, axis=1)
        left = whole.astype(jnp.bfloat16)
        if precise:
            rest = (whole - left.astype(jnp.float32)).astype(jnp.bfloat16)
            left = jnp.concatenate([left, rest], axis=0)
        row = lax.broadcasted_iota(jnp.int32, (SUB, 4 * E), 0)
        out = jnp.zeros((SUB, 4 * E), jnp.float32)
        for k in range(SUB):
            product = jnp.dot(left, ops[k], preferred_element_type=jnp.float32)
            if precise:
                product = product[:SUB] + product[SUB:]
            out = jnp.where(row == k, product, out)
        w = [out[:, side * E : (side + 1) * E] for side in range(4)]
        t = lane_gather(w[0], self.refs["winv"][...]), lane_gather(w[2], self.refs["sinv"][...])
        return w, t

    def send(self, total, ref):
        ref[...] = jnp.broadcast_to(jnp.sum(total, axis=0, keepdims=True), ref.shape)


def from_peers(ref):
    return jnp.sum(ref[...], axis=0, keepdims=True)


def scalar(ref, i):
    return ref[0:1, AT_SCALAR + i : AT_SCALAR + i + 1]


def keep(ref, parts):
    for i, part in enumerate(parts):
        ref[i] = part


def sides(ref):
    return [ref[i] for i in range(ref.shape[0])]


SETUP = ("kw", "ks", "wmap", "smap", "winv", "sinv", "m", "tmw", "tms", "nb_tmw", "nb_me", "nb_tms", "nb_mn")


def setup_kernel(wmap_t, smap_t, m, winv, sinv, tmw, tms):
    lane = lax.broadcasted_iota(jnp.int32, (E, E), 1)
    at = lax.broadcasted_iota(jnp.int32, (E, E), 0).astype(jnp.float32)
    for source, inverse in ((wmap_t, winv), (smap_t, sinv)):
        rows = []
        for k in range(SUB):
            hit = source[:, k : k + 1] == lane
            rows.append(jnp.sum(jnp.where(hit, at, 0.0), axis=0, keepdims=True))
        inverse[...] = jnp.concatenate(rows, axis=0).astype(jnp.int32)
    for r in range(MODES):
        tmw[r] = lane_gather(m[r, :, 0:E], winv[...])
        tms[r] = lane_gather(m[r, :, 2 * E : 3 * E], sinv[...])


def first_kernel(*refs):
    n = len(SETUP)
    local = Local(dict(zip(SETUP, refs[:n])))
    arrived, ops, load_e, load_n, nb_load_e, nb_load_n = refs[n : n + 6]
    out_row, lam, target, w_out, t_out = refs[n + 6 :]
    local.refs["ops"] = ops
    u = local.lift(from_peers(arrived))
    w, t = local.dual(u, False)
    none = jnp.zeros((SUB, LANES), jnp.float32)
    load = local.cross(
        (none, load_e[...], none, load_n[...]), (none, none), (none, nb_load_e[...], none, nb_load_n[...])
    )
    local.send(local.absorb(-local.contributions(w, t), load), out_row)
    keep(lam, (u[1], u[3]))
    keep(target, load)
    keep(w_out, w)
    keep(t_out, t)


def second_kernel(*refs):
    n = len(SETUP)
    local = Local(dict(zip(SETUP, refs[:n])))
    arrived, ops, target, w_in, t_in, nb0, nb1, nb2, nb3 = refs[n : n + 9]
    out_row, coarse, gradient, w_out, t_out = refs[n + 9 :]
    local.refs["ops"] = ops
    row = from_peers(arrived)
    image = local.cross(sides(w_in), sides(t_in), (nb0[...], nb1[...], nb2[...], nb3[...]))
    lifted = local.lift(row)
    g = [target[i] - image[i] - lifted[i] for i in range(4)]
    w, t = local.dual(g, False)
    total = local.contributions(w, t)
    total = local.put(total, g[1] * g[1] + g[3] * g[3], AT_SCALAR)
    total = local.put(total, sum(g[i] * w[i] for i in range(4)), AT_SCALAR + 1)
    local.send(total, out_row)
    coarse[...] = row
    keep(gradient, g)
    keep(w_out, w)
    keep(t_out, t)


def third_kernel(*refs):
    n = len(SETUP)
    local = Local(dict(zip(SETUP, refs[:n])))
    arrived, ops, sums, lam, coarse, gradient, w_in, t_in, nb0, nb1, nb2, nb3 = refs[n : n + 12]
    out_row, lam_out, coarse_out, moved, projected, g_out, w_out, t_out = refs[n + 12 :]
    local.refs["ops"] = ops
    alpha = scalar(sums, 0) / scalar(sums, 1)
    row = from_peers(arrived)
    w1 = sides(w_in)
    image = local.cross(w1, sides(t_in), (nb0[...], nb1[...], nb2[...], nb3[...]))
    lifted = local.lift(row)
    p = [image[i] - lifted[i] for i in range(4)]
    g0 = sides(gradient)
    g = [g0[i] - alpha * p[i] for i in range(4)]
    w, t = local.dual(g, True)
    total = local.contributions(w, t)
    total = local.put(total, g[1] * g[1] + g[3] * g[3], AT_SCALAR)
    total = local.put(total, sum(g[i] * w[i] for i in range(4)), AT_SCALAR + 1)
    total = local.put(total, sum(g0[i] * w[i] + g[i] * w1[i] for i in range(4)), AT_SCALAR + 2)
    local.send(total, out_row)
    keep(lam_out, (lam[0] + alpha * g0[1], lam[1] + alpha * g0[3]))
    coarse_out[...] = coarse[...] - alpha * row
    moved[...] = row
    keep(projected, (p[1], p[3]))
    keep(g_out, (g[1], g[3]))
    keep(w_out, w)
    keep(t_out, t)


def last_kernel(*refs):
    n = len(SETUP)
    local = Local(dict(zip(SETUP, refs[:n])))
    (arrived, sums, sums_next, lam, coarse, moved, g0, projected, g1, w_in, t_in, nb0, nb1, nb2, nb3) = refs[n : n + 15]
    lam_out, g_out, amplitudes = refs[n + 15 :]
    beta = scalar(sums_next, 0) / scalar(sums, 0)
    curve = scalar(sums_next, 1) + beta * (scalar(sums_next, 2) + beta * scalar(sums, 1))
    alpha = scalar(sums_next, 0) / curve
    row = from_peers(arrived)
    image = local.cross(sides(w_in), sides(t_in), (nb0[...], nb1[...], nb2[...], nb3[...]))
    lifted = local.lift(row)
    for i, side in ((0, 1), (1, 3)):
        p = image[side] - lifted[side] + beta * projected[i]
        g_out[i] = g1[i] - alpha * p
        lam_out[i] = lam[i] + alpha * (g1[i] + beta * g0[side])
    amplitudes[...] = alpha * (row + beta * moved[...]) - coarse[...]


def coarse_body(entries, owner, inverse, factor, out, first):
    lane = lax.broadcasted_iota(jnp.int32, (PEERS, LANES), 1)
    group = (
        (lane >= 12).astype(jnp.int32) + (lane >= 24).astype(jnp.int32) + (lane >= 36).astype(jnp.int32)
    )
    within = lane - 12 * group
    if first:
        total = entries
    else:
        from_e = up(lane_gather(entries, jnp.minimum(lane + 12, 127)), 8)
        from_w = down(lane_gather(entries, jnp.minimum(lane + 60, 127)), 8)
        from_n = up(lane_gather(entries, jnp.clip(63 + 3 * group + within, 0, 127)), 1)
        from_s = down(lane_gather(entries, jnp.clip(84 + 3 * group + within, 0, 127)), 1)
        total = entries + jnp.where(lane >= 36, from_e, 0.0) + jnp.where(lane < 12, from_w, 0.0)
        total = total + jnp.where(within >= 9, from_n, 0.0) + jnp.where(within < 3, from_s, 0.0)
    flat = lane_gather(total, owner)
    half = PEERS // 2
    low = lax.broadcasted_iota(jnp.int32, (half, LANES), 1) < 64
    e = jnp.where(low, flat[:half], pltpu.roll(flat[half:], 64, 1))
    z = jnp.zeros((half, LANES), jnp.float32)
    for k in range(BLOCK):
        z = z + factor[k] * jnp.sum(factor[k] * e)
    spread = jnp.concatenate([z, pltpu.roll(z, 64, 1)], axis=0)
    natural = lane_gather(spread, inverse)
    third = lane - AT_S
    g3 = jnp.zeros_like(lane)
    for c in (3, 6, 9):
        g3 = g3 + (third >= c).astype(jnp.int32)
    fourth = lane - AT_N
    g4 = jnp.zeros_like(lane)
    for c in (3, 6, 9):
        g4 = g4 + (fourth >= c).astype(jnp.int32)
    clip = lambda index: jnp.clip(index, 0, 127)
    at_w = down(lane_gather(natural, clip(lane - 12)), 8)
    at_e = up(lane_gather(natural, clip(lane - 60)), 8)
    at_s = down(lane_gather(natural, clip(9 * g3 + 9 + third)), 1)
    at_n = up(lane_gather(natural, clip(9 * g4 + fourth)), 1)
    edge = jnp.where(lane < AT_E, at_w, jnp.where(lane < AT_S, at_e, jnp.where(lane < AT_N, at_s, at_n)))
    out[...] = jnp.where(lane < AT_W, natural, edge)


def coarse_first_kernel(entries, factor, out, owner_out, inverse_out):
    lane = lax.broadcasted_iota(jnp.int32, (PEERS, LANES), 1)
    got = entries[...]
    owner = pltpu.roll(got, LANES - BLOCK, 1).astype(jnp.int32)
    owner = jnp.where(lane < BLOCK, owner, lane)
    inverse = lane
    for j in range(BLOCK):
        inverse = jnp.where(owner[:, j : j + 1] == lane, j, inverse)
    owner_out[...] = owner
    inverse_out[...] = inverse
    coarse_body(got, owner, inverse, factor, out, True)


def coarse_kernel(entries, owner, inverse, factor, out, sums):
    got = entries[...]
    sums[...] = jnp.sum(got, axis=0, keepdims=True)
    coarse_body(got, owner[...], inverse[...], factor, out, False)


def f32(*shape):
    return jax.ShapeDtypeStruct(shape, jnp.float32)


def i32(*shape):
    return jax.ShapeDtypeStruct(shape, jnp.int32)


def call(kernel, outs, *args):
    return pl.pallas_call(
        kernel,
        out_shape=outs,
        in_specs=[pl.BlockSpec(memory_space=pltpu.VMEM)] * len(args),
        out_specs=tuple(pl.BlockSpec(memory_space=pltpu.VMEM) for _ in outs),
        compiler_params=pltpu.CompilerParams(vmem_limit_bytes=40 * 1024 * 1024),
    )(*args)


def exchange(rows):
    return lax.all_to_all(rows, ALL, split_axis=0, concat_axis=0, tiled=True)


def from_next(value, axis):
    n = lax.axis_size(axis)
    return lax.ppermute(value, axis, [(i + 1, i) for i in range(n - 1)])


def from_previous(value, axis):
    n = lax.axis_size(axis)
    return lax.ppermute(value, axis, [(i, i + 1) for i in range(n - 1)])


def halo(w, t):
    return from_next(t[0], GX), from_previous(w[1], GX), from_next(t[1], GY), from_previous(w[3], GY)


def shards(dual_ops, dual_load, mode_images, mode_loads, coarse_factor, west_map, south_map, mode_owner):
    row = jnp.concatenate([mode_loads.reshape(BLOCK), mode_owner.astype(jnp.float32), jnp.zeros(32, jnp.float32)])
    arrived = exchange(jnp.broadcast_to(row[None], (PEERS, LANES)))

    ops = dual_ops.reshape(SUB, 4 * E, 4 * E)
    wmap, smap = west_map.reshape(SUB, E), south_map.reshape(SUB, E)
    m = mode_images.reshape(SUB, MODES, 4 * E).transpose(1, 0, 2)
    load = dual_load.reshape(SUB, 2, E)
    load_e, load_n = load[:, 0], load[:, 1]
    s = lax.broadcasted_iota(jnp.int32, (SUB, LANES), 0)
    kw = jnp.where((lax.axis_index(GX) == 0) & (s < 4), 0.0, 1.0).astype(jnp.float32)
    ks = jnp.where((lax.axis_index(GY) == 0) & (s % 4 == 0), 0.0, 1.0).astype(jnp.float32)
    winv, sinv, tmw, tms = call(
        setup_kernel,
        (i32(SUB, E), i32(SUB, E), f32(MODES, SUB, E), f32(MODES, SUB, E)),
        wmap.T,
        smap.T,
        m,
    )
    nb_tmw, nb_tms = from_next(tmw, GX), from_next(tms, GY)
    nb_e = from_previous(jnp.concatenate([m[:, :, E : 2 * E], load_e[None]], axis=0), GX)
    nb_n = from_previous(jnp.concatenate([m[:, :, 3 * E :], load_n[None]], axis=0), GY)
    setup = (kw, ks, wmap, smap, winv, sinv, m, tmw, tms, nb_tmw, nb_e[:3], nb_tms, nb_n[:3])
    blocks = coarse_factor.reshape(BLOCK, 2, PEERS // 2, BLOCK)
    blocks = jnp.pad(blocks, ((0, 0), (0, 0), (0, 0), (0, 16)))
    factor = jnp.concatenate([blocks[:, 0], blocks[:, 1]], axis=-1)

    rows_out = f32(PEERS, LANES)
    row_out = f32(1, LANES)
    four, two = f32(4, SUB, E), f32(2, SUB, E)

    partial, owner, inverse = call(
        coarse_first_kernel, (rows_out, i32(PEERS, LANES), i32(PEERS, LANES)), arrived, factor
    )
    out_row, lam, target, w, t = call(
        first_kernel,
        (rows_out, two, four, four, two),
        *setup,
        exchange(partial),
        ops,
        load_e,
        load_n,
        nb_e[3],
        nb_n[3],
    )
    near = halo(w, t)
    partial, _ = call(coarse_kernel, (rows_out, row_out), exchange(out_row), owner, inverse, factor)
    out_row, coarse, g0, w1, t1 = call(
        second_kernel, (rows_out, row_out, four, four, two), *setup, exchange(partial), ops, target, w, t, *near
    )
    near = halo(w1, t1)
    partial, sums = call(coarse_kernel, (rows_out, row_out), exchange(out_row), owner, inverse, factor)
    out_row, lam, coarse, moved, projected, g1, w2, t2 = call(
        third_kernel,
        (rows_out, two, row_out, row_out, two, two, four, two),
        *setup,
        exchange(partial),
        ops,
        sums,
        lam,
        coarse,
        g0,
        w1,
        t1,
        *near,
    )
    near = halo(w2, t2)
    partial, sums_next = call(coarse_kernel, (rows_out, row_out), exchange(out_row), owner, inverse, factor)
    lam, g, amplitudes = call(
        last_kernel,
        (two, two, row_out),
        *setup,
        exchange(partial),
        sums,
        sums_next,
        lam,
        coarse,
        moved,
        g0,
        projected,
        g1,
        w2,
        t2,
        *near,
    )

    def owned(value):
        return value.transpose(1, 0, 2).reshape(4, 4, 2, E)

    return owned(lam), owned(g), amplitudes[0, :BLOCK].reshape(4, 4, MODES)


def solution(mesh):
    placed = (
        P(GX, GY, None, None),
        P(GX, GY, None, None),
        P(GX, GY, None, None),
        P(GX, GY, None),
        P(ALL, None),
        P(GX, GY, None),
        P(GX, GY, None),
        P(ALL),
    )
    return jax.shard_map(
        shards,
        mesh=mesh,
        in_specs=placed,
        out_specs=(P(GX, GY, None, None), P(GX, GY, None, None), P(GX, GY, None)),
        check_vma=False,
    )
```

```python
import jax
import jax.numpy as jnp
from jax import lax
from jax.experimental import pallas as pl
from jax.experimental.pallas import tpu as pltpu
from jax.sharding import PartitionSpec as P

GX, GY = "gx", "gy"
ALL = (GX, GY)
SUB = 16
E = 128
MODES = 3
BLOCK = 48
PEERS = 256
LANES = 128

AT_W, AT_E, AT_S, AT_N, AT_EDGE, AT_SCALAR = 48, 60, 72, 84, 96, 104
EDGES_SETUP = (3, 4, 3, 4)
EDGES = (1, 1, 1, 1)


def lane_gather(values, index):
    return jnp.take_along_axis(values, index, axis=1)


def up(values, rows):
    return pltpu.roll(values, values.shape[0] - rows, 0)


def down(values, rows):
    return pltpu.roll(values, rows, 0)


KEEP_W, KEEP_S, M, TMW, TMS, NB_TMW, NB_ME, NB_TMS, NB_MN, TARGET = 0, 1, 2, 14, 17, 20, 23, 26, 29, 32
PACKED = 36
WMAP, SMAP, WINV, SINV = range(4)


class Local:
    def __init__(self, maps, pack):
        self.maps, self.pack = maps, pack
        s = lax.broadcasted_iota(jnp.int32, (SUB, LANES), 0)
        self.lane = lax.broadcasted_iota(jnp.int32, (SUB, LANES), 1)
        self.s, self.x, self.y = s, lax.shift_right_logical(s, 2), lax.bitwise_and(s, 3)

    def own_at(self, r):
        return 3 * self.s + r

    def west_at(self, r):
        return AT_W + 3 * self.y + r

    def east_at(self, r):
        return AT_E + 3 * self.y + r

    def south_at(self, r):
        return AT_S + 3 * self.x + r

    def north_at(self, r):
        return AT_N + 3 * self.x + r

    def cross(self, w, t, nb):
        x, y = self.x, self.y
        nb_tw, nb_we, nb_ts, nb_wn = nb
        east = w[1] - up(jnp.where(x == 0, nb_tw, t[0]), 4)
        north = w[3] - jnp.where(y == 3, down(nb_ts, 3), up(t[1], 1))
        from_west = down(jnp.where(x == 3, nb_we, w[1]), 4)
        from_south = jnp.where(y == 0, up(nb_wn, 3), down(w[3], 1))
        west = self.pack[KEEP_W] * (w[0] - lane_gather(from_west, self.maps[WMAP]))
        south = self.pack[KEEP_S] * (w[2] - lane_gather(from_south, self.maps[SMAP]))
        return west, east, south, north

    def modes(self, r, side):
        return self.pack[M + 4 * r + side]

    def lift(self, row):
        a = jnp.broadcast_to(row, (SUB, LANES))
        pack = self.pack
        w = [0.0] * 4
        t = [0.0] * 2
        nb = [0.0] * 4
        for r in range(MODES):
            own = lane_gather(a, self.own_at(r))
            for side in range(4):
                w[side] += self.modes(r, side) * own
            t[0] += pack[TMW + r] * own
            t[1] += pack[TMS + r] * own
            nb[0] += pack[NB_TMW + r] * lane_gather(a, self.east_at(r))
            nb[1] += pack[NB_ME + r] * lane_gather(a, self.west_at(r))
            nb[2] += pack[NB_TMS + r] * lane_gather(a, self.north_at(r))
            nb[3] += pack[NB_MN + r] * lane_gather(a, self.south_at(r))
        return self.cross(w, t, nb)

    def put(self, total, values, at, rows=None):
        here = self.lane == at
        if rows is not None:
            here = here & rows
        return total + jnp.where(here, jnp.sum(values, axis=1, keepdims=True), 0.0)

    def absorb(self, total, u):
        for r in range(MODES):
            terms = sum(self.modes(r, side) * u[side] for side in range(4))
            total = self.put(total, terms, self.own_at(r))
        return total

    def contributions(self, w, t):
        pack, x, y = self.pack, self.x, self.y
        none = jnp.zeros((SUB, LANES), jnp.float32)
        total = self.absorb(none, self.cross(w, t, (none, none, none, none)))
        to_e, to_w = down(w[1], 4), up(t[0], 4)
        to_n, to_s = up(w[3], 3), down(t[1], 3)
        for r in range(MODES):
            total = self.put(total, -pack[NB_TMW + r] * to_e, self.east_at(r), x == 0)
            total = self.put(total, -pack[NB_ME + r] * to_w, self.west_at(r), x == 3)
            total = self.put(total, -pack[NB_TMS + r] * to_n, self.north_at(r), y == 0)
            total = self.put(total, -pack[NB_MN + r] * to_s, self.south_at(r), y == 3)
        return total

    def dual(self, u, operators, precise):
        whole = jnp.concatenate(u, axis=1)
        left = whole.astype(jnp.bfloat16)
        if precise:
            rest = (whole - left.astype(jnp.float32)).astype(jnp.bfloat16)
            left = jnp.concatenate([left, rest], axis=0)
        row = lax.broadcasted_iota(jnp.int32, (SUB, 4 * E), 0)
        out = jnp.zeros((SUB, 4 * E), jnp.float32)
        for k in range(SUB):
            product = jnp.dot(left, operators.get(k), preferred_element_type=jnp.float32)
            if precise:
                product = product[:SUB] + product[SUB:]
            out = jnp.where(row == k, product, out)
        w = [out[:, side * E : (side + 1) * E] for side in range(4)]
        t = lane_gather(w[0], self.maps[WINV]), lane_gather(w[2], self.maps[SINV])
        return w, t

    def send(self, total, edges, ref):
        send_rows(jnp.sum(total, axis=0, keepdims=True), edges, ref)


class Operators:
    def __init__(self, source, held, arrived):
        self.held = held
        self.copies = []
        for k in range(SUB):
            copy = pltpu.make_async_copy(source.at[k // 4, k % 4], held.at[k], arrived.at[k])
            copy.start()
            self.copies.append(copy)

    def get(self, k):
        self.copies[k].wait()
        return self.held[k]


EDGE_ROWS = ([0, 1, 2, 3], [12, 13, 14, 15], [0, 4, 8, 12], [3, 7, 11, 15])


def send_rows(row, edges, ref):
    at_x, at_y = lax.axis_index(GX), lax.axis_index(GY)
    no_one = (at_x == 0, at_x == lax.axis_size(GX) - 1, at_y == 0, at_y == lax.axis_size(GY) - 1)
    for half in range(2):
        parts = []
        for arrays, rows, none in zip(edges, EDGE_ROWS, no_one):
            for array in arrays:
                for k in (half, half + 2):
                    parts.append(jnp.where(none, 0.0, array[rows[k] : rows[k] + 1]))
        count = len(parts)
        before, rest = jnp.zeros((AT_EDGE, LANES), jnp.float32), LANES - AT_EDGE - count
        parts = [before, *parts, jnp.zeros((rest, LANES), jnp.float32)]
        turned = jnp.concatenate(parts, axis=0).T
        lane = lax.broadcasted_iota(jnp.int32, (LANES, LANES), 1)
        here = (lane >= AT_EDGE) & (lane < AT_EDGE + count)
        ref[half * LANES : (half + 1) * LANES, :] = jnp.where(here, turned, row)


def arrived_edges(ref, counts):
    halves = [ref[half * LANES : (half + 1) * LANES, :].T for half in range(2)]
    s = lax.broadcasted_iota(jnp.int32, (SUB, LANES), 0)
    at = AT_EDGE
    out = []
    for count, place in zip(counts, (lax.bitwise_and(s, 3),) * 2 + (lax.shift_right_logical(s, 2),) * 2):
        arrays = []
        for _ in range(count):
            rows = [halves[k % 2][at + k // 2 : at + k // 2 + 1] for k in range(4)]
            arrays.append(
                jnp.where(place == 0, rows[0], jnp.where(place == 1, rows[1], jnp.where(place == 2, rows[2], rows[3])))
            )
            at += 2
        out.append(arrays)
    return out


def pass_on(entries, lane, counts):
    ends = []
    at = AT_EDGE
    for count in counts:
        at += 2 * count
        ends.append(at)
    moved = jnp.where(lane < ends[2], up(entries, 1), down(entries, 1))
    return jnp.where(lane < ends[0], up(entries, 8), jnp.where(lane < ends[1], down(entries, 8), moved))


def from_peers(ref):
    return jnp.sum(ref[...], axis=0, keepdims=True)


def scalar(ref, i):
    return ref[0:1, AT_SCALAR + i : AT_SCALAR + i + 1]


def keep(ref, *parts):
    for i, part in enumerate(parts):
        ref[i] = jnp.broadcast_to(part, (SUB, LANES))


LOAD_E, LOAD_N, KEPT = 20, 21, 22


def start_kernel(loads, owner, west_map, south_map, images, load, out, maps, kept):
    lane = lax.broadcasted_iota(jnp.int32, (E, E), 1)
    at = lax.broadcasted_iota(jnp.int32, (E, E), 0)
    for source, direct, inverse in ((west_map, WMAP, WINV), (south_map, SMAP, SINV)):
        rows = jnp.concatenate([source[x] for x in range(4)], axis=0)
        maps[direct] = rows
        columns = jnp.concatenate([rows, jnp.zeros((E - SUB, E), jnp.int32)], axis=0).T
        found = []
        for k in range(SUB):
            hit = columns[:, k : k + 1] == lane
            found.append(jnp.sum(jnp.where(hit, at, 0), axis=0, keepdims=True))
        maps[inverse] = jnp.concatenate(found, axis=0)
    s = lax.broadcasted_iota(jnp.int32, (SUB, LANES), 0)
    first_x, first_y = lax.axis_index(GX) == 0, lax.axis_index(GY) == 0
    kept[KEEP_W] = jnp.where(first_x & (s < 4), 0.0, 1.0)
    kept[KEEP_S] = jnp.where(first_y & (lax.bitwise_and(s, 3) == 0), 0.0, 1.0)
    for r in range(MODES):
        whole = jnp.concatenate([images[x, r] for x in range(4)], axis=0)
        for side in range(4):
            kept[M + 4 * r + side] = whole[:, side * E : (side + 1) * E]
        kept[TMW + r] = lane_gather(whole[:, :E], maps[WINV])
        kept[TMS + r] = lane_gather(whole[:, 2 * E : 3 * E], maps[SINV])
    kept[LOAD_E] = jnp.concatenate([load[k // 4, k % 4, 0:1, :] for k in range(SUB)], axis=0)
    kept[LOAD_N] = jnp.concatenate([load[k // 4, k % 4, 1:2, :] for k in range(SUB)], axis=0)

    x = lax.broadcasted_iota(jnp.int32, (8, LANES), 0)
    lane8 = lax.broadcasted_iota(jnp.int32, (8, LANES), 1)
    off = lane8 - 12 * x
    y = sum((off >= c).astype(jnp.int32) for c in (3, 6, 9))
    natural = jnp.zeros((8, LANES), jnp.float32)
    for r in range(MODES):
        block = jnp.concatenate([loads[r], jnp.zeros((4, 4), jnp.float32)], axis=0)
        block = jnp.concatenate([block, jnp.zeros((8, LANES - 4), jnp.float32)], axis=1)
        here = (off >= 0) & (off < 12) & (off - 3 * y == r) & (x < 4)
        natural = natural + jnp.where(here, lane_gather(block, y), 0.0)
    natural = jnp.broadcast_to(jnp.sum(natural, axis=0, keepdims=True), (8, LANES))
    owner_row = jnp.concatenate([owner[...], jnp.zeros((1, LANES - BLOCK), jnp.int32)], axis=1)
    flat = lane_gather(natural, jnp.broadcast_to(owner_row, (8, LANES)))[0:1]
    hit = (jnp.broadcast_to(owner_row, (E, E)).T == lane) & (at < BLOCK)
    inverse = jnp.sum(jnp.where(hit, at, 0), axis=0, keepdims=True).astype(jnp.float32)
    lane1 = lax.broadcasted_iota(jnp.int32, (1, LANES), 1)
    row = jnp.where(lane1 < BLOCK, flat, pltpu.roll(jnp.broadcast_to(inverse, (8, LANES)), BLOCK, 1)[0:1])
    three = lambda first, step: [kept[first + step * r] for r in range(MODES)]
    edges = (
        three(TMW, 1),
        three(M + 1, 4) + [kept[LOAD_E]],
        three(TMS, 1),
        three(M + 3, 4) + [kept[LOAD_N]],
    )
    send_rows(row, edges, out)


def pack_constants(arrived, maps, kept, pack):
    nb_tw, nb_e, nb_ts, nb_n = arrived_edges(arrived, EDGES_SETUP)
    for i in range(LOAD_E):
        pack[i] = kept[i]
    for r in range(MODES):
        pack[NB_TMW + r] = nb_tw[r]
        pack[NB_ME + r] = nb_e[r]
        pack[NB_TMS + r] = nb_ts[r]
        pack[NB_MN + r] = nb_n[r]
    local = Local(maps, pack)
    none = jnp.zeros((SUB, LANES), jnp.float32)
    load = (none, kept[LOAD_E], none, kept[LOAD_N])
    target = local.cross(load, (none, none), (none, nb_e[MODES], none, nb_n[MODES]))
    for side in range(4):
        pack[TARGET + side] = target[side]
    return local, local.absorb(none, target)


W, T, LAM, G0, COARSE, P1, G1, MOVED = 0, 4, 6, 8, 12, 13, 15, 17


def product_out(local, total, state, w, t, out_row):
    keep(state, *w, *t)
    local.send(total, ([t[0]], [w[1]], [t[1]], [w[3]]), out_row)


def image_of(local, arrived, state):
    w = [state[W + i] for i in range(4)]
    near = [arrays[0] for arrays in arrived_edges(arrived, EDGES)]
    return w, local.cross(w, [state[T], state[T + 1]], near)


def first_kernel(arrived, maps, kept, dual_ops, out_row, state, pack, *rest):
    operators = Operators(dual_ops, *rest)
    local, entries = pack_constants(arrived, maps, kept, pack)
    u = local.lift(from_peers(arrived))
    w, t = local.dual(u, operators, False)
    product_out(local, entries - local.contributions(w, t), state, w, t, out_row)
    state[LAM] = u[1]
    state[LAM + 1] = u[3]


def second_kernel(arrived, maps, pack, dual_ops, before, out_row, state, *rest):
    operators = Operators(dual_ops, *rest)
    local = Local(maps, pack)
    row = from_peers(arrived)
    _, image = image_of(local, arrived, before)
    lifted = local.lift(row)
    g = [pack[TARGET + i] - image[i] - lifted[i] for i in range(4)]
    w, t = local.dual(g, operators, False)
    total = local.contributions(w, t)
    total = local.put(total, g[1] * g[1] + g[3] * g[3], AT_SCALAR)
    total = local.put(total, sum(g[i] * w[i] for i in range(4)), AT_SCALAR + 1)
    product_out(local, total, state, w, t, out_row)
    state[LAM] = before[LAM]
    state[LAM + 1] = before[LAM + 1]
    for i in range(4):
        state[G0 + i] = g[i]
    state[COARSE] = jnp.broadcast_to(row, (SUB, LANES))


def third_kernel(arrived, maps, pack, dual_ops, before, sums, out_row, state, *rest):
    operators = Operators(dual_ops, *rest)
    local = Local(maps, pack)
    alpha = scalar(sums, 0) / scalar(sums, 1)
    row = from_peers(arrived)
    w1, image = image_of(local, arrived, before)
    lifted = local.lift(row)
    p = [image[i] - lifted[i] for i in range(4)]
    g0 = [before[G0 + i] for i in range(4)]
    g = [g0[i] - alpha * p[i] for i in range(4)]
    w, t = local.dual(g, operators, True)
    total = local.contributions(w, t)
    total = local.put(total, g[1] * g[1] + g[3] * g[3], AT_SCALAR)
    total = local.put(total, sum(g[i] * w[i] for i in range(4)), AT_SCALAR + 1)
    total = local.put(total, sum(g0[i] * w[i] + g[i] * w1[i] for i in range(4)), AT_SCALAR + 2)
    product_out(local, total, state, w, t, out_row)
    state[LAM] = before[LAM] + alpha * g0[1]
    state[LAM + 1] = before[LAM + 1] + alpha * g0[3]
    for i in range(4):
        state[G0 + i] = g0[i]
    state[COARSE] = before[COARSE] - alpha * row
    for i, side in ((0, 1), (1, 3)):
        state[P1 + i] = p[side]
        state[G1 + i] = g[side]
    state[MOVED] = jnp.broadcast_to(row, (SUB, LANES))


def last_kernel(arrived, maps, pack, before, sums, sums_next, lam_out, g_out, amplitudes):
    local = Local(maps, pack)
    beta = scalar(sums_next, 0) / scalar(sums, 0)
    curve = scalar(sums_next, 1) + beta * (scalar(sums_next, 2) + beta * scalar(sums, 1))
    alpha = scalar(sums_next, 0) / curve
    row = from_peers(arrived)
    _, image = image_of(local, arrived, before)
    lifted = local.lift(row)
    for i, side in ((0, 1), (1, 3)):
        p = image[side] - lifted[side] + beta * before[P1 + i]
        g_out[:, i, :] = before[G1 + i] - alpha * p
        lam_out[:, i, :] = before[LAM + i] + alpha * (before[G1 + i] + beta * before[G0 + side])
    a = alpha * (row + beta * before[MOVED]) - before[COARSE]
    x = lax.broadcasted_iota(jnp.int32, (SUB, LANES), 0)
    for r in range(MODES):
        at = jnp.minimum(12 * x + 3 * local.lane + r, 127)
        amplitudes[r] = lane_gather(a, at)[:4, :4]


def third_of(lane, base):
    off = lane - base
    return sum((off >= c).astype(jnp.int32) for c in (3, 6, 9)), off


def coarse_body(entries, owner, inverse, factor, out, first=False):
    lane = lax.broadcasted_iota(jnp.int32, (PEERS, LANES), 1)
    group = sum((lane >= c).astype(jnp.int32) for c in (12, 24, 36))
    within = lane - 12 * group
    clip = lambda index: jnp.clip(index, 0, LANES - 1)
    total = entries
    if not first:
        from_e = up(lane_gather(entries, clip(lane + 12)), 8)
        from_w = down(lane_gather(entries, clip(lane + 60)), 8)
        from_n = up(lane_gather(entries, clip(63 + 3 * group + within)), 1)
        from_s = down(lane_gather(entries, clip(84 + 3 * group + within)), 1)
        total = total + jnp.where(lane >= 36, from_e, 0.0) + jnp.where(lane < 12, from_w, 0.0)
        total = total + jnp.where(within >= 9, from_n, 0.0) + jnp.where(within < 3, from_s, 0.0)
    placed = lane_gather(total, owner)
    q = lax.broadcasted_iota(jnp.int32, (8, LANES), 0)
    within = lax.bitwise_and(lax.broadcasted_iota(jnp.int32, (8, LANES), 1) - BLOCK * q, LANES - 1)
    column = jnp.where(within < BLOCK, lax.shift_right_logical(BLOCK * q + within, 7), -1)
    here = [column == j for j in range(3)]
    groups = PEERS // 8
    tile = lambda g, j: factor[:, (3 * g + j) * LANES : (3 * g + j + 1) * LANES]
    y = jnp.zeros((BLOCK, LANES), jnp.float32)
    for g in range(groups):
        rows = placed[8 * g : 8 * g + 8]
        for j in range(3):
            y = y + tile(g, j) * jnp.sum(jnp.where(here[j], rows, 0.0), axis=0, keepdims=True)
    y = jnp.broadcast_to(jnp.sum(y, axis=1, keepdims=True), (BLOCK, LANES))
    spread = []
    for g in range(groups):
        z = [jnp.sum(tile(g, j) * y, axis=0, keepdims=True) for j in range(3)]
        spread.append(jnp.where(here[0], z[0], jnp.where(here[1], z[1], z[2])))
    natural = lane_gather(jnp.concatenate(spread, axis=0), inverse)
    g3, off3 = third_of(lane, AT_S)
    g4, off4 = third_of(lane, AT_N)
    at_w = down(lane_gather(natural, clip(lane - 12)), 8)
    at_e = up(lane_gather(natural, clip(lane - 60)), 8)
    at_s = down(lane_gather(natural, clip(9 * g3 + 9 + off3)), 1)
    at_n = up(lane_gather(natural, clip(9 * g4 + off4)), 1)
    edge = jnp.where(lane < AT_E, at_w, jnp.where(lane < AT_S, at_e, jnp.where(lane < AT_N, at_s, at_n)))
    edges = pass_on(entries, lane, EDGES_SETUP if first else EDGES)
    out[...] = jnp.where(lane < AT_W, natural, jnp.where(lane < AT_EDGE, edge, edges))


def places():
    lane = lax.broadcasted_iota(jnp.int32, (PEERS, LANES), 1)
    return lane, BLOCK * lax.bitwise_and(lax.broadcasted_iota(jnp.int32, (PEERS, LANES), 0), 7)


def coarse_first_kernel(entries, factor, out, inverse_out):
    lane, start = places()
    got = entries[...]
    inverse = jnp.where(lane < BLOCK, pltpu.roll(got, LANES - BLOCK, 1).astype(jnp.int32), lane)
    inverse = lax.bitwise_and(inverse + start, LANES - 1)
    inverse_out[...] = inverse
    coarse_body(got, lax.bitwise_and(lane - start, LANES - 1), inverse, factor, out, True)


def owner_kernel(inverse, owner_out):
    lane, start = places()
    places_of = lax.bitwise_and(inverse[...] - start, LANES - 1)
    owner = lane
    for k in range(BLOCK):
        owner = jnp.where(places_of[:, k : k + 1] == lane, k, owner)
    owner_out[...] = lane_gather(owner, lax.bitwise_and(lane - start, LANES - 1))


def coarse_kernel(entries, owner, inverse, factor, out, sums):
    got = entries[...]
    sums[...] = jnp.sum(got, axis=0, keepdims=True)
    coarse_body(got, owner[...], inverse[...], factor, out, False)


def f32(*shape):
    return jax.ShapeDtypeStruct(shape, jnp.float32)


def i32(*shape):
    return jax.ShapeDtypeStruct(shape, jnp.int32)


def call(kernel, outs, *args, operators=None):
    specs = [pl.BlockSpec(memory_space=pltpu.HBM) if i == operators else pl.BlockSpec() for i in range(len(args))]
    scratch = []
    if operators is not None:
        scratch = [pltpu.VMEM((SUB, 4 * E, 4 * E), jnp.bfloat16), pltpu.SemaphoreType.DMA((SUB,))]
    return pl.pallas_call(
        kernel,
        out_shape=outs,
        in_specs=specs,
        out_specs=tuple(pl.BlockSpec() for _ in outs),
        scratch_shapes=scratch,
        compiler_params=pltpu.CompilerParams(vmem_limit_bytes=(24 if operators is None else 56) * 1024 * 1024),
    )(*args)


def exchange(rows):
    return lax.all_to_all(rows, ALL, split_axis=0, concat_axis=0, tiled=True)


def shards(dual_ops, dual_load, mode_images, mode_loads, coarse_factor, west_map, south_map, mode_owner):
    rows, row, indices = f32(PEERS, LANES), f32(1, LANES), i32(PEERS, LANES)
    sent, maps, kept = call(
        start_kernel,
        (rows, i32(4, SUB, E), f32(KEPT, SUB, E)),
        mode_loads.transpose(2, 0, 1),
        mode_owner.reshape(1, BLOCK),
        west_map,
        south_map,
        mode_images.transpose(0, 2, 1, 3),
        dual_load,
    )
    partial, inverse = call(coarse_first_kernel, (rows, indices), exchange(sent), coarse_factor)
    arrived = exchange(partial)
    (owner,) = call(owner_kernel, (indices,), inverse)

    def solve(sent):
        partial, sums = call(coarse_kernel, (rows, row), exchange(sent), owner, inverse, coarse_factor)
        return exchange(partial), sums

    sent, state, pack = call(
        first_kernel, (rows, f32(8, SUB, E), f32(PACKED, SUB, E)), arrived, maps, kept, dual_ops, operators=3
    )
    arrived, _ = solve(sent)
    sent, state = call(
        second_kernel, (rows, f32(13, SUB, E)), arrived, maps, pack, dual_ops, state, operators=3
    )
    arrived, sums = solve(sent)
    sent, state = call(
        third_kernel, (rows, f32(18, SUB, E)), arrived, maps, pack, dual_ops, state, sums, operators=3
    )
    arrived, sums_next = solve(sent)
    lam, gradient, amplitudes = call(
        last_kernel,
        (f32(SUB, 2, E), f32(SUB, 2, E), f32(MODES, 4, 4)),
        arrived,
        maps,
        pack,
        state,
        sums,
        sums_next,
    )
    return lam.reshape(4, 4, 2, E), gradient.reshape(4, 4, 2, E), amplitudes.transpose(1, 2, 0)


def solution(mesh):
    placed = (
        P(GX, GY, None, None),
        P(GX, GY, None, None),
        P(GX, GY, None, None),
        P(GX, GY, None),
        P(ALL, None),
        P(GX, GY, None),
        P(GX, GY, None),
        P(ALL),
    )
    return jax.shard_map(
        shards,
        mesh=mesh,
        in_specs=placed,
        out_specs=(P(GX, GY, None, None), P(GX, GY, None, None), P(GX, GY, None)),
        check_vma=False,
    )
```

```python
import jax
import jax.numpy as jnp
from jax import lax
from jax.experimental import pallas as pl
from jax.experimental.pallas import tpu as pltpu
from jax.sharding import PartitionSpec as P

GX, GY = "gx", "gy"
ALL = (GX, GY)
SUB = 16
E = 128
MODES = 3
BLOCK = 48
PEERS = 256
LANES = 128

AT_W, AT_E, AT_S, AT_N, AT_EDGE, AT_SCALAR = 48, 60, 72, 84, 96, 104
EDGES_SETUP = (3, 4, 3, 4)
EDGES = (1, 1, 1, 1)


def lane_gather(values, index):
    return jnp.take_along_axis(values, index, axis=1)


def up(values, rows):
    return pltpu.roll(values, values.shape[0] - rows, 0)


def down(values, rows):
    return pltpu.roll(values, rows, 0)


KEEP_W, KEEP_S, M, TMW, TMS, NB_TMW, NB_ME, NB_TMS, NB_MN, TARGET = 0, 1, 2, 14, 17, 20, 23, 26, 29, 32
MAPS, PACKED = 36, 40
WMAP, SMAP, WINV, SINV = range(4)


class Local:
    def __init__(self, pack):
        self.pack = pack
        self.maps = [pack[MAPS + i].astype(jnp.int32) for i in range(4)]
        s = lax.broadcasted_iota(jnp.int32, (SUB, LANES), 0)
        self.lane = lax.broadcasted_iota(jnp.int32, (SUB, LANES), 1)
        self.s, self.x, self.y = s, lax.shift_right_logical(s, 2), lax.bitwise_and(s, 3)

    def own_at(self, r):
        return 3 * self.s + r

    def west_at(self, r):
        return AT_W + 3 * self.y + r

    def east_at(self, r):
        return AT_E + 3 * self.y + r

    def south_at(self, r):
        return AT_S + 3 * self.x + r

    def north_at(self, r):
        return AT_N + 3 * self.x + r

    def cross(self, w, t, nb):
        x, y = self.x, self.y
        nb_tw, nb_we, nb_ts, nb_wn = nb
        east = w[1] - up(jnp.where(x == 0, nb_tw, t[0]), 4)
        north = w[3] - jnp.where(y == 3, down(nb_ts, 3), up(t[1], 1))
        from_west = down(jnp.where(x == 3, nb_we, w[1]), 4)
        from_south = jnp.where(y == 0, up(nb_wn, 3), down(w[3], 1))
        west = self.pack[KEEP_W] * (w[0] - lane_gather(from_west, self.maps[WMAP]))
        south = self.pack[KEEP_S] * (w[2] - lane_gather(from_south, self.maps[SMAP]))
        return west, east, south, north

    def modes(self, r, side):
        return self.pack[M + 4 * r + side]

    def lift(self, row):
        a = jnp.broadcast_to(row, (SUB, LANES))
        pack = self.pack
        w = [0.0] * 4
        t = [0.0] * 2
        nb = [0.0] * 4
        for r in range(MODES):
            own = lane_gather(a, self.own_at(r))
            for side in range(4):
                w[side] += self.modes(r, side) * own
            t[0] += pack[TMW + r] * own
            t[1] += pack[TMS + r] * own
            nb[0] += pack[NB_TMW + r] * lane_gather(a, self.east_at(r))
            nb[1] += pack[NB_ME + r] * lane_gather(a, self.west_at(r))
            nb[2] += pack[NB_TMS + r] * lane_gather(a, self.north_at(r))
            nb[3] += pack[NB_MN + r] * lane_gather(a, self.south_at(r))
        return self.cross(w, t, nb)

    def put(self, total, values, at, rows=None):
        here = self.lane == at
        if rows is not None:
            here = here & rows
        return total + jnp.where(here, jnp.sum(values, axis=1, keepdims=True), 0.0)

    def absorb(self, total, u):
        for r in range(MODES):
            terms = sum(self.modes(r, side) * u[side] for side in range(4))
            total = self.put(total, terms, self.own_at(r))
        return total

    def contributions(self, w, t):
        pack, x, y = self.pack, self.x, self.y
        none = jnp.zeros((SUB, LANES), jnp.float32)
        total = self.absorb(none, self.cross(w, t, (none, none, none, none)))
        to_e, to_w = down(w[1], 4), up(t[0], 4)
        to_n, to_s = up(w[3], 3), down(t[1], 3)
        for r in range(MODES):
            total = self.put(total, -pack[NB_TMW + r] * to_e, self.east_at(r), x == 0)
            total = self.put(total, -pack[NB_ME + r] * to_w, self.west_at(r), x == 3)
            total = self.put(total, -pack[NB_TMS + r] * to_n, self.north_at(r), y == 0)
            total = self.put(total, -pack[NB_MN + r] * to_s, self.south_at(r), y == 3)
        return total

    def dual(self, u, operators, precise):
        whole = jnp.concatenate(u, axis=1)
        left = whole.astype(jnp.bfloat16)
        if precise:
            rest = (whole - left.astype(jnp.float32)).astype(jnp.bfloat16)
            left = jnp.concatenate([left, rest], axis=0)
        row = lax.broadcasted_iota(jnp.int32, (SUB, 4 * E), 0)
        out = jnp.zeros((SUB, 4 * E), jnp.float32)
        for k in range(SUB):
            product = operators.times(k, left)
            if precise:
                product = product[:SUB] + product[SUB:]
            out = jnp.where(row == k, product, out)
        w = [out[:, side * E : (side + 1) * E] for side in range(4)]
        t = lane_gather(w[0], self.maps[WINV]), lane_gather(w[2], self.maps[SINV])
        return w, t

    def send(self, total, edges, ref):
        send_rows(jnp.sum(total, axis=0, keepdims=True), edges, ref)


class Operators:
    def __init__(self, source, held, arrived):
        self.held = held
        self.copies = []
        for k in range(SUB):
            copy = pltpu.make_async_copy(source.at[k // 4, k % 4], held.at[k], arrived.at[k])
            copy.start()
            self.copies.append(copy)

    def times(self, k, left):
        self.copies[k].wait()
        return jnp.dot(left, self.held[k], preferred_element_type=jnp.float32)


EDGE_ROWS = ([0, 1, 2, 3], [12, 13, 14, 15], [0, 4, 8, 12], [3, 7, 11, 15])


def send_rows(row, edges, ref):
    at_x, at_y = lax.axis_index(GX), lax.axis_index(GY)
    no_one = (at_x == 0, at_x == lax.axis_size(GX) - 1, at_y == 0, at_y == lax.axis_size(GY) - 1)
    for half in range(2):
        parts = []
        for arrays, rows, none in zip(edges, EDGE_ROWS, no_one):
            for array in arrays:
                for k in (half, half + 2):
                    parts.append(jnp.where(none, 0.0, array[rows[k] : rows[k] + 1]))
        count = len(parts)
        before, rest = jnp.zeros((AT_EDGE, LANES), jnp.float32), LANES - AT_EDGE - count
        parts = [before, *parts, jnp.zeros((rest, LANES), jnp.float32)]
        turned = jnp.concatenate(parts, axis=0).T
        lane = lax.broadcasted_iota(jnp.int32, (LANES, LANES), 1)
        here = (lane >= AT_EDGE) & (lane < AT_EDGE + count)
        ref[half * LANES : (half + 1) * LANES, :] = jnp.where(here, turned, row)


def arrived_edges(ref, counts):
    halves = [ref[half * LANES : (half + 1) * LANES, :].T for half in range(2)]
    s = lax.broadcasted_iota(jnp.int32, (SUB, LANES), 0)
    at = AT_EDGE
    out = []
    for count, place in zip(counts, (lax.bitwise_and(s, 3),) * 2 + (lax.shift_right_logical(s, 2),) * 2):
        arrays = []
        for _ in range(count):
            rows = [halves[k % 2][at + k // 2 : at + k // 2 + 1] for k in range(4)]
            arrays.append(
                jnp.where(place == 0, rows[0], jnp.where(place == 1, rows[1], jnp.where(place == 2, rows[2], rows[3])))
            )
            at += 2
        out.append(arrays)
    return out


def pass_on(entries, lane, counts):
    ends = []
    at = AT_EDGE
    for count in counts:
        at += 2 * count
        ends.append(at)
    moved = jnp.where(lane < ends[2], up(entries, 1), down(entries, 1))
    return jnp.where(lane < ends[0], up(entries, 8), jnp.where(lane < ends[1], down(entries, 8), moved))


def from_peers(ref):
    return jnp.sum(ref[...], axis=0, keepdims=True)


def scalar(ref, i):
    return ref[0:1, AT_SCALAR + i : AT_SCALAR + i + 1]


def keep(ref, *parts):
    for i, part in enumerate(parts):
        ref[i] = jnp.broadcast_to(part, (SUB, LANES))


LOAD_E, LOAD_N, KEPT_MAPS, KEPT = 20, 21, 22, 26


def start_kernel(loads, owner, west_map, south_map, images, load, out, kept):
    lane = lax.broadcasted_iota(jnp.int32, (E, E), 1)
    at = lax.broadcasted_iota(jnp.int32, (E, E), 0)
    inverses = []
    for source, direct, inverse in ((west_map, WMAP, WINV), (south_map, SMAP, SINV)):
        rows = jnp.concatenate([source[x] for x in range(4)], axis=0)
        kept[KEPT_MAPS + direct] = rows.astype(jnp.float32)
        columns = jnp.concatenate([rows, jnp.zeros((E - SUB, E), jnp.int32)], axis=0).T
        found = []
        for k in range(SUB):
            hit = columns[:, k : k + 1] == lane
            found.append(jnp.sum(jnp.where(hit, at, 0), axis=0, keepdims=True))
        inverses.append(jnp.concatenate(found, axis=0))
        kept[KEPT_MAPS + inverse] = inverses[-1].astype(jnp.float32)
    s = lax.broadcasted_iota(jnp.int32, (SUB, LANES), 0)
    first_x, first_y = lax.axis_index(GX) == 0, lax.axis_index(GY) == 0
    kept[KEEP_W] = jnp.where(first_x & (s < 4), 0.0, 1.0)
    kept[KEEP_S] = jnp.where(first_y & (lax.bitwise_and(s, 3) == 0), 0.0, 1.0)
    for r in range(MODES):
        whole = jnp.concatenate([images[x, r] for x in range(4)], axis=0)
        for side in range(4):
            kept[M + 4 * r + side] = whole[:, side * E : (side + 1) * E]
        kept[TMW + r] = lane_gather(whole[:, :E], inverses[0])
        kept[TMS + r] = lane_gather(whole[:, 2 * E : 3 * E], inverses[1])
    kept[LOAD_E] = jnp.concatenate([load[k // 4, k % 4, 0:1, :] for k in range(SUB)], axis=0)
    kept[LOAD_N] = jnp.concatenate([load[k // 4, k % 4, 1:2, :] for k in range(SUB)], axis=0)

    x = lax.broadcasted_iota(jnp.int32, (8, LANES), 0)
    lane8 = lax.broadcasted_iota(jnp.int32, (8, LANES), 1)
    off = lane8 - 12 * x
    y = sum((off >= c).astype(jnp.int32) for c in (3, 6, 9))
    natural = jnp.zeros((8, LANES), jnp.float32)
    for r in range(MODES):
        block = jnp.concatenate([loads[r], jnp.zeros((4, 4), jnp.float32)], axis=0)
        block = jnp.concatenate([block, jnp.zeros((8, LANES - 4), jnp.float32)], axis=1)
        here = (off >= 0) & (off < 12) & (off - 3 * y == r) & (x < 4)
        natural = natural + jnp.where(here, lane_gather(block, y), 0.0)
    natural = jnp.broadcast_to(jnp.sum(natural, axis=0, keepdims=True), (8, LANES))
    owner_row = jnp.concatenate([owner[...], jnp.zeros((1, LANES - BLOCK), jnp.int32)], axis=1)
    flat = lane_gather(natural, jnp.broadcast_to(owner_row, (8, LANES)))[0:1]
    hit = (jnp.broadcast_to(owner_row, (E, E)).T == lane) & (at < BLOCK)
    inverse = jnp.sum(jnp.where(hit, at, 0), axis=0, keepdims=True).astype(jnp.float32)
    lane1 = lax.broadcasted_iota(jnp.int32, (1, LANES), 1)
    row = jnp.where(lane1 < BLOCK, flat, pltpu.roll(jnp.broadcast_to(inverse, (8, LANES)), BLOCK, 1)[0:1])
    three = lambda first, step: [kept[first + step * r] for r in range(MODES)]
    edges = (
        three(TMW, 1),
        three(M + 1, 4) + [kept[LOAD_E]],
        three(TMS, 1),
        three(M + 3, 4) + [kept[LOAD_N]],
    )
    send_rows(row, edges, out)


def pack_constants(arrived, kept, pack):
    nb_tw, nb_e, nb_ts, nb_n = arrived_edges(arrived, EDGES_SETUP)
    for i in range(LOAD_E):
        pack[i] = kept[i]
    for i in range(4):
        pack[MAPS + i] = kept[KEPT_MAPS + i]
    for r in range(MODES):
        pack[NB_TMW + r] = nb_tw[r]
        pack[NB_ME + r] = nb_e[r]
        pack[NB_TMS + r] = nb_ts[r]
        pack[NB_MN + r] = nb_n[r]
    local = Local(pack)
    none = jnp.zeros((SUB, LANES), jnp.float32)
    load = (none, kept[LOAD_E], none, kept[LOAD_N])
    target = local.cross(load, (none, none), (none, nb_e[MODES], none, nb_n[MODES]))
    for side in range(4):
        pack[TARGET + side] = target[side]
    return local, local.absorb(none, target)


W, T, LAM, G0, COARSE, P1, G1, MOVED = 0, 4, 6, 8, 12, 13, 15, 17


def product_out(local, total, state, w, t, out_row):
    keep(state, *w, *t)
    local.send(total, ([t[0]], [w[1]], [t[1]], [w[3]]), out_row)


def image_of(local, arrived, state):
    w = [state[W + i] for i in range(4)]
    near = [arrays[0] for arrays in arrived_edges(arrived, EDGES)]
    return w, local.cross(w, [state[T], state[T + 1]], near)


def first_kernel(arrived, kept, dual_ops, out_row, state, pack, *rest):
    operators = Operators(dual_ops, *rest)
    local, entries = pack_constants(arrived, kept, pack)
    u = local.lift(from_peers(arrived))
    w, t = local.dual(u, operators, False)
    product_out(local, entries - local.contributions(w, t), state, w, t, out_row)
    state[LAM] = u[1]
    state[LAM + 1] = u[3]


def second_kernel(arrived, pack, dual_ops, before, out_row, state, *rest):
    operators = Operators(dual_ops, *rest)
    local = Local(pack)
    row = from_peers(arrived)
    _, image = image_of(local, arrived, before)
    lifted = local.lift(row)
    g = [pack[TARGET + i] - image[i] - lifted[i] for i in range(4)]
    w, t = local.dual(g, operators, False)
    total = local.contributions(w, t)
    total = local.put(total, g[1] * g[1] + g[3] * g[3], AT_SCALAR)
    total = local.put(total, sum(g[i] * w[i] for i in range(4)), AT_SCALAR + 1)
    product_out(local, total, state, w, t, out_row)
    state[LAM] = before[LAM]
    state[LAM + 1] = before[LAM + 1]
    for i in range(4):
        state[G0 + i] = g[i]
    state[COARSE] = jnp.broadcast_to(row, (SUB, LANES))


def third_kernel(arrived, pack, dual_ops, before, sums, out_row, state, *rest):
    operators = Operators(dual_ops, *rest)
    local = Local(pack)
    alpha = scalar(sums, 0) / scalar(sums, 1)
    row = from_peers(arrived)
    w1, image = image_of(local, arrived, before)
    lifted = local.lift(row)
    p = [image[i] - lifted[i] for i in range(4)]
    g0 = [before[G0 + i] for i in range(4)]
    g = [g0[i] - alpha * p[i] for i in range(4)]
    w, t = local.dual(g, operators, True)
    total = local.contributions(w, t)
    total = local.put(total, g[1] * g[1] + g[3] * g[3], AT_SCALAR)
    total = local.put(total, sum(g[i] * w[i] for i in range(4)), AT_SCALAR + 1)
    total = local.put(total, sum(g0[i] * w[i] + g[i] * w1[i] for i in range(4)), AT_SCALAR + 2)
    product_out(local, total, state, w, t, out_row)
    state[LAM] = before[LAM] + alpha * g0[1]
    state[LAM + 1] = before[LAM + 1] + alpha * g0[3]
    for i in range(4):
        state[G0 + i] = g0[i]
    state[COARSE] = before[COARSE] - alpha * row
    for i, side in ((0, 1), (1, 3)):
        state[P1 + i] = p[side]
        state[G1 + i] = g[side]
    state[MOVED] = jnp.broadcast_to(row, (SUB, LANES))


def last_kernel(arrived, pack, before, sums, sums_next, lam_out, g_out, amplitudes):
    local = Local(pack)
    beta = scalar(sums_next, 0) / scalar(sums, 0)
    curve = scalar(sums_next, 1) + beta * (scalar(sums_next, 2) + beta * scalar(sums, 1))
    alpha = scalar(sums_next, 0) / curve
    row = from_peers(arrived)
    _, image = image_of(local, arrived, before)
    lifted = local.lift(row)
    for i, side in ((0, 1), (1, 3)):
        p = image[side] - lifted[side] + beta * before[P1 + i]
        g_out[:, i, :] = before[G1 + i] - alpha * p
        lam_out[:, i, :] = before[LAM + i] + alpha * (before[G1 + i] + beta * before[G0 + side])
    a = alpha * (row + beta * before[MOVED]) - before[COARSE]
    x = lax.broadcasted_iota(jnp.int32, (SUB, LANES), 0)
    for r in range(MODES):
        at = jnp.minimum(12 * x + 3 * local.lane + r, 127)
        amplitudes[r] = lane_gather(a, at)[:4, :4]


def third_of(lane, base):
    off = lane - base
    return sum((off >= c).astype(jnp.int32) for c in (3, 6, 9)), off


def coarse_body(entries, owner, inverse, factor, out, first=False):
    lane = lax.broadcasted_iota(jnp.int32, (PEERS, LANES), 1)
    group = sum((lane >= c).astype(jnp.int32) for c in (12, 24, 36))
    within = lane - 12 * group
    clip = lambda index: jnp.clip(index, 0, LANES - 1)
    total = entries
    if not first:
        from_e = up(lane_gather(entries, clip(lane + 12)), 8)
        from_w = down(lane_gather(entries, clip(lane + 60)), 8)
        from_n = up(lane_gather(entries, clip(63 + 3 * group + within)), 1)
        from_s = down(lane_gather(entries, clip(84 + 3 * group + within)), 1)
        total = total + jnp.where(lane >= 36, from_e, 0.0) + jnp.where(lane < 12, from_w, 0.0)
        total = total + jnp.where(within >= 9, from_n, 0.0) + jnp.where(within < 3, from_s, 0.0)
    placed = lane_gather(total, owner)
    q = lax.broadcasted_iota(jnp.int32, (8, LANES), 0)
    within = lax.bitwise_and(lax.broadcasted_iota(jnp.int32, (8, LANES), 1) - BLOCK * q, LANES - 1)
    column = jnp.where(within < BLOCK, lax.shift_right_logical(BLOCK * q + within, 7), -1)
    here = [column == j for j in range(3)]
    groups = PEERS // 8
    tile = lambda g, j: factor[:, (3 * g + j) * LANES : (3 * g + j + 1) * LANES]
    y = jnp.zeros((BLOCK, LANES), jnp.float32)
    for g in range(groups):
        rows = placed[8 * g : 8 * g + 8]
        for j in range(3):
            y = y + tile(g, j) * jnp.sum(jnp.where(here[j], rows, 0.0), axis=0, keepdims=True)
    y = jnp.broadcast_to(jnp.sum(y, axis=1, keepdims=True), (BLOCK, LANES))
    spread = []
    for g in range(groups):
        z = [jnp.sum(tile(g, j) * y, axis=0, keepdims=True) for j in range(3)]
        spread.append(jnp.where(here[0], z[0], jnp.where(here[1], z[1], z[2])))
    natural = lane_gather(jnp.concatenate(spread, axis=0), inverse)
    g3, off3 = third_of(lane, AT_S)
    g4, off4 = third_of(lane, AT_N)
    at_w = down(lane_gather(natural, clip(lane - 12)), 8)
    at_e = up(lane_gather(natural, clip(lane - 60)), 8)
    at_s = down(lane_gather(natural, clip(9 * g3 + 9 + off3)), 1)
    at_n = up(lane_gather(natural, clip(9 * g4 + off4)), 1)
    edge = jnp.where(lane < AT_E, at_w, jnp.where(lane < AT_S, at_e, jnp.where(lane < AT_N, at_s, at_n)))
    edges = pass_on(entries, lane, EDGES_SETUP if first else EDGES)
    out[...] = jnp.where(lane < AT_W, natural, jnp.where(lane < AT_EDGE, edge, edges))


def places():
    lane = lax.broadcasted_iota(jnp.int32, (PEERS, LANES), 1)
    return lane, BLOCK * lax.bitwise_and(lax.broadcasted_iota(jnp.int32, (PEERS, LANES), 0), 7)


def coarse_first_kernel(entries, factor, out, inverse_out):
    lane, start = places()
    got = entries[...]
    inverse = jnp.where(lane < BLOCK, pltpu.roll(got, LANES - BLOCK, 1).astype(jnp.int32), lane)
    inverse = lax.bitwise_and(inverse + start, LANES - 1)
    inverse_out[...] = inverse
    coarse_body(got, lax.bitwise_and(lane - start, LANES - 1), inverse, factor, out, True)


def owner_kernel(inverse, owner_out):
    lane, start = places()
    places_of = lax.bitwise_and(inverse[...] - start, LANES - 1)
    owner = lane
    for k in range(BLOCK):
        owner = jnp.where(places_of[:, k : k + 1] == lane, k, owner)
    owner_out[...] = lane_gather(owner, lax.bitwise_and(lane - start, LANES - 1))


def coarse_kernel(entries, owner, inverse, factor, out, *sums):
    got = entries[...]
    for ref in sums:
        ref[...] = jnp.sum(got, axis=0, keepdims=True)
    coarse_body(got, owner[...], inverse[...], factor, out, False)


def f32(*shape):
    return jax.ShapeDtypeStruct(shape, jnp.float32)


def i32(*shape):
    return jax.ShapeDtypeStruct(shape, jnp.int32)


def call(kernel, outs, *args, operators=None, megabytes=16):
    specs = [pl.BlockSpec(memory_space=pltpu.HBM) if i == operators else pl.BlockSpec() for i in range(len(args))]
    scratch = []
    if operators is not None:
        megabytes = 50
        scratch = [
            pltpu.VMEM((SUB, 4 * E, 4 * E), jnp.bfloat16),
            pltpu.SemaphoreType.DMA((SUB,)),
        ]
    return pl.pallas_call(
        kernel,
        out_shape=outs,
        in_specs=specs,
        out_specs=tuple(pl.BlockSpec() for _ in outs),
        scratch_shapes=scratch,
        compiler_params=pltpu.CompilerParams(vmem_limit_bytes=megabytes * 1024 * 1024),
    )(*args)


def settle_kernel(value, out):
    out[...] = value[...]


def after(first, *values):
    return lax.optimization_barrier((first, values))


def exchange(rows):
    return lax.all_to_all(rows, ALL, split_axis=0, concat_axis=0, tiled=True)


def shards(dual_ops, dual_load, mode_images, mode_loads, coarse_factor, west_map, south_map, mode_owner):
    rows, row, indices = f32(PEERS, LANES), f32(1, LANES), i32(PEERS, LANES)
    sent, kept = call(
        start_kernel,
        (rows, f32(KEPT, SUB, E)),
        mode_loads.transpose(2, 0, 1),
        mode_owner.reshape(1, BLOCK),
        west_map,
        south_map,
        mode_images.transpose(0, 2, 1, 3),
        dual_load,
        megabytes=60,
    )
    partial, inverse = call(coarse_first_kernel, (rows, indices), exchange(sent), coarse_factor)
    partial, (kept,) = after(partial, kept)
    arrived = exchange(partial)
    (kept,) = call(settle_kernel, (f32(KEPT, SUB, E),), kept)
    (owner,) = call(owner_kernel, (indices,), inverse)

    def solve(sent, *sums):
        partial, *sums = call(coarse_kernel, (rows, *sums), exchange(sent), owner, inverse, coarse_factor)
        return exchange(partial), *sums

    sent, state, pack = call(
        first_kernel, (rows, f32(8, SUB, E), f32(PACKED, SUB, E)), arrived, kept, dual_ops, operators=2
    )
    (arrived,) = solve(sent)
    sent, state = call(
        second_kernel, (rows, f32(13, SUB, E)), arrived, pack, dual_ops, state, operators=2
    )
    arrived, sums = solve(sent, row)
    sent, state = call(
        third_kernel, (rows, f32(18, SUB, E)), arrived, pack, dual_ops, state, sums, operators=2
    )
    arrived, sums_next = solve(sent, row)
    lam, gradient, amplitudes = call(
        last_kernel,
        (f32(SUB, 2, E), f32(SUB, 2, E), f32(MODES, 4, 4)),
        arrived,
        pack,
        state,
        sums,
        sums_next,
    )
    return lam.reshape(4, 4, 2, E), gradient.reshape(4, 4, 2, E), amplitudes.transpose(1, 2, 0)


def solution(mesh):
    placed = (
        P(GX, GY, None, None),
        P(GX, GY, None, None),
        P(GX, GY, None, None),
        P(GX, GY, None),
        P(ALL, None),
        P(GX, GY, None),
        P(GX, GY, None),
        P(ALL),
    )
    return jax.shard_map(
        shards,
        mesh=mesh,
        in_specs=placed,
        out_specs=(P(GX, GY, None, None), P(GX, GY, None, None), P(GX, GY, None)),
        check_vma=False,
    )
```

```python
import jax
import jax.numpy as jnp
from jax import lax
from jax.experimental import pallas as pl
from jax.experimental.pallas import tpu as pltpu
from jax.sharding import PartitionSpec as P

GX, GY = "gx", "gy"
ALL = (GX, GY)
SUB = 16
E = 128
MODES = 3
BLOCK = 48
PEERS = 256
LANES = 128

AT_W, AT_E, AT_S, AT_N, AT_EDGE, AT_SCALAR = 48, 60, 72, 84, 96, 104
EDGES_SETUP = (3, 4, 3, 4)
EDGES = (1, 1, 1, 1)


def lane_gather(values, index):
    return jnp.take_along_axis(values, index, axis=1)


def up(values, rows):
    return pltpu.roll(values, values.shape[0] - rows, 0)


def down(values, rows):
    return pltpu.roll(values, rows, 0)


KEEP_W, KEEP_S, M, TMW, TMS, NB_TMW, NB_ME, NB_TMS, NB_MN, TARGET = 0, 1, 2, 14, 17, 20, 23, 26, 29, 32
MAPS, PACKED = 36, 40
WMAP, SMAP, WINV, SINV = range(4)


class Local:
    def __init__(self, pack):
        self.pack = pack
        self.maps = [pack[MAPS + i].astype(jnp.int32) for i in range(4)]
        s = lax.broadcasted_iota(jnp.int32, (SUB, LANES), 0)
        self.lane = lax.broadcasted_iota(jnp.int32, (SUB, LANES), 1)
        self.s, self.x, self.y = s, lax.shift_right_logical(s, 2), lax.bitwise_and(s, 3)

    def own_at(self, r):
        return 3 * self.s + r

    def west_at(self, r):
        return AT_W + 3 * self.y + r

    def east_at(self, r):
        return AT_E + 3 * self.y + r

    def south_at(self, r):
        return AT_S + 3 * self.x + r

    def north_at(self, r):
        return AT_N + 3 * self.x + r

    def cross(self, w, t, nb):
        x, y = self.x, self.y
        nb_tw, nb_we, nb_ts, nb_wn = nb
        east = w[1] - up(jnp.where(x == 0, nb_tw, t[0]), 4)
        north = w[3] - jnp.where(y == 3, down(nb_ts, 3), up(t[1], 1))
        from_west = down(jnp.where(x == 3, nb_we, w[1]), 4)
        from_south = jnp.where(y == 0, up(nb_wn, 3), down(w[3], 1))
        west = self.pack[KEEP_W] * (w[0] - lane_gather(from_west, self.maps[WMAP]))
        south = self.pack[KEEP_S] * (w[2] - lane_gather(from_south, self.maps[SMAP]))
        return west, east, south, north

    def modes(self, r, side):
        return self.pack[M + 4 * r + side]

    def lift(self, row):
        a = jnp.broadcast_to(row, (SUB, LANES))
        pack = self.pack
        w = [0.0] * 4
        t = [0.0] * 2
        nb = [0.0] * 4
        for r in range(MODES):
            own = lane_gather(a, self.own_at(r))
            for side in range(4):
                w[side] += self.modes(r, side) * own
            t[0] += pack[TMW + r] * own
            t[1] += pack[TMS + r] * own
            nb[0] += pack[NB_TMW + r] * lane_gather(a, self.east_at(r))
            nb[1] += pack[NB_ME + r] * lane_gather(a, self.west_at(r))
            nb[2] += pack[NB_TMS + r] * lane_gather(a, self.north_at(r))
            nb[3] += pack[NB_MN + r] * lane_gather(a, self.south_at(r))
        return self.cross(w, t, nb)

    def put(self, total, values, at, rows=None):
        here = self.lane == at
        if rows is not None:
            here = here & rows
        return total + jnp.where(here, jnp.sum(values, axis=1, keepdims=True), 0.0)

    def absorb(self, total, u):
        for r in range(MODES):
            terms = sum(self.modes(r, side) * u[side] for side in range(4))
            total = self.put(total, terms, self.own_at(r))
        return total

    def contributions(self, w, t):
        pack, x, y = self.pack, self.x, self.y
        none = jnp.zeros((SUB, LANES), jnp.float32)
        total = self.absorb(none, self.cross(w, t, (none, none, none, none)))
        to_e, to_w = down(w[1], 4), up(t[0], 4)
        to_n, to_s = up(w[3], 3), down(t[1], 3)
        for r in range(MODES):
            total = self.put(total, -pack[NB_TMW + r] * to_e, self.east_at(r), x == 0)
            total = self.put(total, -pack[NB_ME + r] * to_w, self.west_at(r), x == 3)
            total = self.put(total, -pack[NB_TMS + r] * to_n, self.north_at(r), y == 0)
            total = self.put(total, -pack[NB_MN + r] * to_s, self.south_at(r), y == 3)
        return total

    def dual(self, u, operators, precise):
        whole = jnp.concatenate(u, axis=1)
        left = whole.astype(jnp.bfloat16)
        if precise:
            rest = (whole - left.astype(jnp.float32)).astype(jnp.bfloat16)
            left = jnp.concatenate([left, rest], axis=0)
        row = lax.broadcasted_iota(jnp.int32, (SUB, 4 * E), 0)
        out = jnp.zeros((SUB, 4 * E), jnp.float32)
        for k in range(SUB):
            product = operators.times(k, left)
            if precise:
                product = product[:SUB] + product[SUB:]
            out = jnp.where(row == k, product, out)
        w = [out[:, side * E : (side + 1) * E] for side in range(4)]
        t = lane_gather(w[0], self.maps[WINV]), lane_gather(w[2], self.maps[SINV])
        return w, t

    def send(self, total, edges, ref):
        send_rows(jnp.sum(total, axis=0, keepdims=True), edges, ref)


class Operators:
    def __init__(self, source, held, arrived):
        self.held = held
        self.copies = []
        for k in range(SUB):
            copy = pltpu.make_async_copy(source.at[k // 4, k % 4], held.at[k], arrived.at[k])
            copy.start()
            self.copies.append(copy)

    def times(self, k, left):
        self.copies[k].wait()
        return jnp.dot(left, self.held[k], preferred_element_type=jnp.float32)


class Held:
    def __init__(self, source):
        self.source = source

    def times(self, k, left):
        return jnp.dot(left, self.source[k // 4, k % 4], preferred_element_type=jnp.float32)


EDGE_ROWS = ([0, 1, 2, 3], [12, 13, 14, 15], [0, 4, 8, 12], [3, 7, 11, 15])


def send_rows(row, edges, ref):
    at_x, at_y = lax.axis_index(GX), lax.axis_index(GY)
    no_one = (at_x == 0, at_x == lax.axis_size(GX) - 1, at_y == 0, at_y == lax.axis_size(GY) - 1)
    for half in range(2):
        parts = []
        for arrays, rows, none in zip(edges, EDGE_ROWS, no_one):
            for array in arrays:
                for k in (half, half + 2):
                    parts.append(jnp.where(none, 0.0, array[rows[k] : rows[k] + 1]))
        count = len(parts)
        before, rest = jnp.zeros((AT_EDGE, LANES), jnp.float32), LANES - AT_EDGE - count
        parts = [before, *parts, jnp.zeros((rest, LANES), jnp.float32)]
        turned = jnp.concatenate(parts, axis=0).T
        lane = lax.broadcasted_iota(jnp.int32, (LANES, LANES), 1)
        here = (lane >= AT_EDGE) & (lane < AT_EDGE + count)
        ref[half * LANES : (half + 1) * LANES, :] = jnp.where(here, turned, row)


def arrived_edges(ref, counts):
    halves = [ref[half * LANES : (half + 1) * LANES, :].T for half in range(2)]
    s = lax.broadcasted_iota(jnp.int32, (SUB, LANES), 0)
    at = AT_EDGE
    out = []
    for count, place in zip(counts, (lax.bitwise_and(s, 3),) * 2 + (lax.shift_right_logical(s, 2),) * 2):
        arrays = []
        for _ in range(count):
            rows = [halves[k % 2][at + k // 2 : at + k // 2 + 1] for k in range(4)]
            arrays.append(
                jnp.where(place == 0, rows[0], jnp.where(place == 1, rows[1], jnp.where(place == 2, rows[2], rows[3])))
            )
            at += 2
        out.append(arrays)
    return out


def pass_on(entries, lane, counts):
    ends = []
    at = AT_EDGE
    for count in counts:
        at += 2 * count
        ends.append(at)
    moved = jnp.where(lane < ends[2], up(entries, 1), down(entries, 1))
    return jnp.where(lane < ends[0], up(entries, 8), jnp.where(lane < ends[1], down(entries, 8), moved))


def from_peers(ref):
    return jnp.sum(ref[...], axis=0, keepdims=True)


def scalar(ref, i):
    return ref[0:1, AT_SCALAR + i : AT_SCALAR + i + 1]


def keep(ref, *parts):
    for i, part in enumerate(parts):
        ref[i] = jnp.broadcast_to(part, (SUB, LANES))


LOAD_E, LOAD_N, KEPT_MAPS, KEPT = 20, 21, 22, 26


def start_kernel(loads, owner, west_map, south_map, images, load, out, kept):
    lane = lax.broadcasted_iota(jnp.int32, (E, E), 1)
    at = lax.broadcasted_iota(jnp.int32, (E, E), 0)
    inverses = []
    for source, direct, inverse in ((west_map, WMAP, WINV), (south_map, SMAP, SINV)):
        rows = jnp.concatenate([source[x] for x in range(4)], axis=0)
        kept[KEPT_MAPS + direct] = rows.astype(jnp.float32)
        columns = jnp.concatenate([rows, jnp.zeros((E - SUB, E), jnp.int32)], axis=0).T
        found = []
        for k in range(SUB):
            hit = columns[:, k : k + 1] == lane
            found.append(jnp.sum(jnp.where(hit, at, 0), axis=0, keepdims=True))
        inverses.append(jnp.concatenate(found, axis=0))
        kept[KEPT_MAPS + inverse] = inverses[-1].astype(jnp.float32)
    s = lax.broadcasted_iota(jnp.int32, (SUB, LANES), 0)
    first_x, first_y = lax.axis_index(GX) == 0, lax.axis_index(GY) == 0
    kept[KEEP_W] = jnp.where(first_x & (s < 4), 0.0, 1.0)
    kept[KEEP_S] = jnp.where(first_y & (lax.bitwise_and(s, 3) == 0), 0.0, 1.0)
    for r in range(MODES):
        whole = jnp.concatenate([images[x, r] for x in range(4)], axis=0)
        for side in range(4):
            kept[M + 4 * r + side] = whole[:, side * E : (side + 1) * E]
        kept[TMW + r] = lane_gather(whole[:, :E], inverses[0])
        kept[TMS + r] = lane_gather(whole[:, 2 * E : 3 * E], inverses[1])
    kept[LOAD_E] = jnp.concatenate([load[k // 4, k % 4, 0:1, :] for k in range(SUB)], axis=0)
    kept[LOAD_N] = jnp.concatenate([load[k // 4, k % 4, 1:2, :] for k in range(SUB)], axis=0)

    x = lax.broadcasted_iota(jnp.int32, (8, LANES), 0)
    lane8 = lax.broadcasted_iota(jnp.int32, (8, LANES), 1)
    off = lane8 - 12 * x
    y = sum((off >= c).astype(jnp.int32) for c in (3, 6, 9))
    natural = jnp.zeros((8, LANES), jnp.float32)
    for r in range(MODES):
        block = jnp.concatenate([loads[r], jnp.zeros((4, 4), jnp.float32)], axis=0)
        block = jnp.concatenate([block, jnp.zeros((8, LANES - 4), jnp.float32)], axis=1)
        here = (off >= 0) & (off < 12) & (off - 3 * y == r) & (x < 4)
        natural = natural + jnp.where(here, lane_gather(block, y), 0.0)
    natural = jnp.broadcast_to(jnp.sum(natural, axis=0, keepdims=True), (8, LANES))
    owner_row = jnp.concatenate([owner[...], jnp.zeros((1, LANES - BLOCK), jnp.int32)], axis=1)
    flat = lane_gather(natural, jnp.broadcast_to(owner_row, (8, LANES)))[0:1]
    hit = (jnp.broadcast_to(owner_row, (E, E)).T == lane) & (at < BLOCK)
    inverse = jnp.sum(jnp.where(hit, at, 0), axis=0, keepdims=True).astype(jnp.float32)
    lane1 = lax.broadcasted_iota(jnp.int32, (1, LANES), 1)
    row = jnp.where(lane1 < BLOCK, flat, pltpu.roll(jnp.broadcast_to(inverse, (8, LANES)), BLOCK, 1)[0:1])
    three = lambda first, step: [kept[first + step * r] for r in range(MODES)]
    edges = (
        three(TMW, 1),
        three(M + 1, 4) + [kept[LOAD_E]],
        three(TMS, 1),
        three(M + 3, 4) + [kept[LOAD_N]],
    )
    send_rows(row, edges, out)


def pack_constants(arrived, kept, pack):
    nb_tw, nb_e, nb_ts, nb_n = arrived_edges(arrived, EDGES_SETUP)
    for i in range(LOAD_E):
        pack[i] = kept[i]
    for i in range(4):
        pack[MAPS + i] = kept[KEPT_MAPS + i]
    for r in range(MODES):
        pack[NB_TMW + r] = nb_tw[r]
        pack[NB_ME + r] = nb_e[r]
        pack[NB_TMS + r] = nb_ts[r]
        pack[NB_MN + r] = nb_n[r]
    local = Local(pack)
    none = jnp.zeros((SUB, LANES), jnp.float32)
    load = (none, kept[LOAD_E], none, kept[LOAD_N])
    target = local.cross(load, (none, none), (none, nb_e[MODES], none, nb_n[MODES]))
    for side in range(4):
        pack[TARGET + side] = target[side]
    return local, local.absorb(none, target)


W, T, LAM, G0, COARSE, P1, G1, MOVED = 0, 4, 6, 8, 12, 13, 15, 17


def product_out(local, total, state, w, t, out_row):
    keep(state, *w, *t)
    local.send(total, ([t[0]], [w[1]], [t[1]], [w[3]]), out_row)


def image_of(local, arrived, state):
    w = [state[W + i] for i in range(4)]
    near = [arrays[0] for arrays in arrived_edges(arrived, EDGES)]
    return w, local.cross(w, [state[T], state[T + 1]], near)


def first_kernel(arrived, kept, dual_ops, out_row, state, pack, *rest):
    operators = Operators(dual_ops, *rest)
    local, entries = pack_constants(arrived, kept, pack)
    u = local.lift(from_peers(arrived))
    w, t = local.dual(u, operators, False)
    product_out(local, entries - local.contributions(w, t), state, w, t, out_row)
    state[LAM] = u[1]
    state[LAM + 1] = u[3]


def second_kernel(arrived, pack, dual_ops, before, out_row, state):
    operators = Held(dual_ops)
    local = Local(pack)
    row = from_peers(arrived)
    _, image = image_of(local, arrived, before)
    lifted = local.lift(row)
    g = [pack[TARGET + i] - image[i] - lifted[i] for i in range(4)]
    w, t = local.dual(g, operators, False)
    total = local.contributions(w, t)
    total = local.put(total, g[1] * g[1] + g[3] * g[3], AT_SCALAR)
    total = local.put(total, sum(g[i] * w[i] for i in range(4)), AT_SCALAR + 1)
    product_out(local, total, state, w, t, out_row)
    state[LAM] = before[LAM]
    state[LAM + 1] = before[LAM + 1]
    for i in range(4):
        state[G0 + i] = g[i]
    state[COARSE] = jnp.broadcast_to(row, (SUB, LANES))


def third_kernel(arrived, pack, dual_ops, before, sums, out_row, state):
    operators = Held(dual_ops)
    local = Local(pack)
    alpha = scalar(sums, 0) / scalar(sums, 1)
    row = from_peers(arrived)
    w1, image = image_of(local, arrived, before)
    lifted = local.lift(row)
    p = [image[i] - lifted[i] for i in range(4)]
    g0 = [before[G0 + i] for i in range(4)]
    g = [g0[i] - alpha * p[i] for i in range(4)]
    w, t = local.dual(g, operators, True)
    total = local.contributions(w, t)
    total = local.put(total, g[1] * g[1] + g[3] * g[3], AT_SCALAR)
    total = local.put(total, sum(g[i] * w[i] for i in range(4)), AT_SCALAR + 1)
    total = local.put(total, sum(g0[i] * w[i] + g[i] * w1[i] for i in range(4)), AT_SCALAR + 2)
    product_out(local, total, state, w, t, out_row)
    state[LAM] = before[LAM] + alpha * g0[1]
    state[LAM + 1] = before[LAM + 1] + alpha * g0[3]
    for i in range(4):
        state[G0 + i] = g0[i]
    state[COARSE] = before[COARSE] - alpha * row
    for i, side in ((0, 1), (1, 3)):
        state[P1 + i] = p[side]
        state[G1 + i] = g[side]
    state[MOVED] = jnp.broadcast_to(row, (SUB, LANES))


def last_kernel(arrived, pack, before, sums, sums_next, lam_out, g_out, amplitudes):
    local = Local(pack)
    beta = scalar(sums_next, 0) / scalar(sums, 0)
    curve = scalar(sums_next, 1) + beta * (scalar(sums_next, 2) + beta * scalar(sums, 1))
    alpha = scalar(sums_next, 0) / curve
    row = from_peers(arrived)
    _, image = image_of(local, arrived, before)
    lifted = local.lift(row)
    for i, side in ((0, 1), (1, 3)):
        p = image[side] - lifted[side] + beta * before[P1 + i]
        g_out[:, i, :] = before[G1 + i] - alpha * p
        lam_out[:, i, :] = before[LAM + i] + alpha * (before[G1 + i] + beta * before[G0 + side])
    a = alpha * (row + beta * before[MOVED]) - before[COARSE]
    x = lax.broadcasted_iota(jnp.int32, (SUB, LANES), 0)
    for r in range(MODES):
        at = jnp.minimum(12 * x + 3 * local.lane + r, 127)
        amplitudes[r] = lane_gather(a, at)[:4, :4]


def third_of(lane, base):
    off = lane - base
    return sum((off >= c).astype(jnp.int32) for c in (3, 6, 9)), off


def coarse_body(entries, owner, inverse, factor, out, first=False):
    lane = lax.broadcasted_iota(jnp.int32, (PEERS, LANES), 1)
    group = sum((lane >= c).astype(jnp.int32) for c in (12, 24, 36))
    within = lane - 12 * group
    clip = lambda index: jnp.clip(index, 0, LANES - 1)
    total = entries
    if not first:
        from_e = up(lane_gather(entries, clip(lane + 12)), 8)
        from_w = down(lane_gather(entries, clip(lane + 60)), 8)
        from_n = up(lane_gather(entries, clip(63 + 3 * group + within)), 1)
        from_s = down(lane_gather(entries, clip(84 + 3 * group + within)), 1)
        total = total + jnp.where(lane >= 36, from_e, 0.0) + jnp.where(lane < 12, from_w, 0.0)
        total = total + jnp.where(within >= 9, from_n, 0.0) + jnp.where(within < 3, from_s, 0.0)
    placed = lane_gather(total, owner)
    q = lax.broadcasted_iota(jnp.int32, (8, LANES), 0)
    within = lax.bitwise_and(lax.broadcasted_iota(jnp.int32, (8, LANES), 1) - BLOCK * q, LANES - 1)
    column = jnp.where(within < BLOCK, lax.shift_right_logical(BLOCK * q + within, 7), -1)
    here = [column == j for j in range(3)]
    groups = PEERS // 8
    tile = lambda g, j: factor[:, (3 * g + j) * LANES : (3 * g + j + 1) * LANES]
    y = jnp.zeros((BLOCK, LANES), jnp.float32)
    for g in range(groups):
        rows = placed[8 * g : 8 * g + 8]
        for j in range(3):
            y = y + tile(g, j) * jnp.sum(jnp.where(here[j], rows, 0.0), axis=0, keepdims=True)
    y = jnp.broadcast_to(jnp.sum(y, axis=1, keepdims=True), (BLOCK, LANES))
    spread = []
    for g in range(groups):
        z = [jnp.sum(tile(g, j) * y, axis=0, keepdims=True) for j in range(3)]
        spread.append(jnp.where(here[0], z[0], jnp.where(here[1], z[1], z[2])))
    natural = lane_gather(jnp.concatenate(spread, axis=0), inverse)
    g3, off3 = third_of(lane, AT_S)
    g4, off4 = third_of(lane, AT_N)
    at_w = down(lane_gather(natural, clip(lane - 12)), 8)
    at_e = up(lane_gather(natural, clip(lane - 60)), 8)
    at_s = down(lane_gather(natural, clip(9 * g3 + 9 + off3)), 1)
    at_n = up(lane_gather(natural, clip(9 * g4 + off4)), 1)
    edge = jnp.where(lane < AT_E, at_w, jnp.where(lane < AT_S, at_e, jnp.where(lane < AT_N, at_s, at_n)))
    edges = pass_on(entries, lane, EDGES_SETUP if first else EDGES)
    out[...] = jnp.where(lane < AT_W, natural, jnp.where(lane < AT_EDGE, edge, edges))


def places():
    lane = lax.broadcasted_iota(jnp.int32, (PEERS, LANES), 1)
    return lane, BLOCK * lax.bitwise_and(lax.broadcasted_iota(jnp.int32, (PEERS, LANES), 0), 7)


def coarse_first_kernel(entries, factor, out, inverse_out):
    lane, start = places()
    got = entries[...]
    inverse = jnp.where(lane < BLOCK, pltpu.roll(got, LANES - BLOCK, 1).astype(jnp.int32), lane)
    inverse = lax.bitwise_and(inverse + start, LANES - 1)
    inverse_out[...] = inverse
    coarse_body(got, lax.bitwise_and(lane - start, LANES - 1), inverse, factor, out, True)


def owner_kernel(inverse, owner_out):
    lane, start = places()
    places_of = lax.bitwise_and(inverse[...] - start, LANES - 1)
    owner = lane
    for k in range(BLOCK):
        owner = jnp.where(places_of[:, k : k + 1] == lane, k, owner)
    owner_out[...] = lane_gather(owner, lax.bitwise_and(lane - start, LANES - 1))


def coarse_kernel(entries, owner, inverse, factor, out, *sums):
    got = entries[...]
    for ref in sums:
        ref[...] = jnp.sum(got, axis=0, keepdims=True)
    coarse_body(got, owner[...], inverse[...], factor, out, False)


def f32(*shape):
    return jax.ShapeDtypeStruct(shape, jnp.float32)


def i32(*shape):
    return jax.ShapeDtypeStruct(shape, jnp.int32)


def call(kernel, outs, *args, operators=None, megabytes=16):
    specs = [pl.BlockSpec(memory_space=pltpu.HBM) if i == operators else pl.BlockSpec() for i in range(len(args))]
    scratch = []
    if operators is not None:
        megabytes = 50
        scratch = [
            pltpu.VMEM((SUB, 4 * E, 4 * E), jnp.bfloat16),
            pltpu.SemaphoreType.DMA((SUB,)),
        ]
    return pl.pallas_call(
        kernel,
        out_shape=outs,
        in_specs=specs,
        out_specs=tuple(pl.BlockSpec() for _ in outs),
        scratch_shapes=scratch,
        compiler_params=pltpu.CompilerParams(vmem_limit_bytes=megabytes * 1024 * 1024),
    )(*args)


def settle_kernel(value, inverse, out, owner):
    out[...] = value[...]
    owner_kernel(inverse, owner)


def after(first, *values):
    return lax.optimization_barrier((first, values))


def exchange(rows):
    return lax.all_to_all(rows, ALL, split_axis=0, concat_axis=0, tiled=True)


def shards(dual_ops, dual_load, mode_images, mode_loads, coarse_factor, west_map, south_map, mode_owner):
    rows, row, indices = f32(PEERS, LANES), f32(1, LANES), i32(PEERS, LANES)
    sent, kept = call(
        start_kernel,
        (rows, f32(KEPT, SUB, E)),
        mode_loads.transpose(2, 0, 1),
        mode_owner.reshape(1, BLOCK),
        west_map,
        south_map,
        mode_images.transpose(0, 2, 1, 3),
        dual_load,
        megabytes=60,
    )
    partial, inverse = call(coarse_first_kernel, (rows, indices), exchange(sent), coarse_factor)
    partial, (kept,) = after(partial, kept)
    arrived = exchange(partial)
    kept, owner = call(settle_kernel, (f32(KEPT, SUB, E), indices), kept, inverse)

    def solve(sent, *sums):
        partial, *sums = call(coarse_kernel, (rows, *sums), exchange(sent), owner, inverse, coarse_factor)
        return exchange(partial), *sums

    sent, state, pack = call(
        first_kernel, (rows, f32(8, SUB, E), f32(PACKED, SUB, E)), arrived, kept, dual_ops, operators=2
    )
    (arrived,) = solve(sent)
    sent, state = call(
        second_kernel, (rows, f32(13, SUB, E)), arrived, pack, dual_ops, state
    )
    arrived, sums = solve(sent, row)
    sent, state = call(
        third_kernel, (rows, f32(18, SUB, E)), arrived, pack, dual_ops, state, sums
    )
    arrived, sums_next = solve(sent, row)
    lam, gradient, amplitudes = call(
        last_kernel,
        (f32(SUB, 2, E), f32(SUB, 2, E), f32(MODES, 4, 4)),
        arrived,
        pack,
        state,
        sums,
        sums_next,
    )
    return lam.reshape(4, 4, 2, E), gradient.reshape(4, 4, 2, E), amplitudes.transpose(1, 2, 0)


def solution(mesh):
    placed = (
        P(GX, GY, None, None),
        P(GX, GY, None, None),
        P(GX, GY, None, None),
        P(GX, GY, None),
        P(ALL, None),
        P(GX, GY, None),
        P(GX, GY, None),
        P(ALL),
    )
    return jax.shard_map(
        shards,
        mesh=mesh,
        in_specs=placed,
        out_specs=(P(GX, GY, None, None), P(GX, GY, None, None), P(GX, GY, None)),
        check_vma=False,
    )
```

```python
import jax
import jax.numpy as jnp
from jax import lax
from jax.experimental import pallas as pl
from jax.experimental.pallas import tpu as pltpu
from jax.sharding import PartitionSpec as P

GX, GY = "gx", "gy"
ALL = (GX, GY)
SUB = 16
E = 128
MODES = 3
BLOCK = 48
PEERS = 256
LANES = 128

AT_W, AT_E, AT_S, AT_N, AT_EDGE, AT_SCALAR = 48, 60, 72, 84, 96, 104
EDGES_SETUP = (3, 4, 3, 4)
EDGES = (1, 1, 1, 1)


def lane_gather(values, index):
    return jnp.take_along_axis(values, index, axis=1)


def up(values, rows):
    return pltpu.roll(values, values.shape[0] - rows, 0)


def down(values, rows):
    return pltpu.roll(values, rows, 0)


KEEP_W, KEEP_S, M, TMW, TMS, NB_TMW, NB_ME, NB_TMS, NB_MN, TARGET = 0, 1, 2, 14, 17, 20, 23, 26, 29, 32
MAPS, PACKED = 36, 40
WMAP, SMAP, WINV, SINV = range(4)


class Local:
    def __init__(self, pack):
        self.pack = pack
        self.maps = [pack[MAPS + i].astype(jnp.int32) for i in range(4)]
        s = lax.broadcasted_iota(jnp.int32, (SUB, LANES), 0)
        self.lane = lax.broadcasted_iota(jnp.int32, (SUB, LANES), 1)
        self.s, self.x, self.y = s, lax.shift_right_logical(s, 2), lax.bitwise_and(s, 3)

    def own_at(self, r):
        return 3 * self.s + r

    def west_at(self, r):
        return AT_W + 3 * self.y + r

    def east_at(self, r):
        return AT_E + 3 * self.y + r

    def south_at(self, r):
        return AT_S + 3 * self.x + r

    def north_at(self, r):
        return AT_N + 3 * self.x + r

    def cross(self, w, t, nb):
        x, y = self.x, self.y
        nb_tw, nb_we, nb_ts, nb_wn = nb
        east = w[1] - up(jnp.where(x == 0, nb_tw, t[0]), 4)
        north = w[3] - jnp.where(y == 3, down(nb_ts, 3), up(t[1], 1))
        from_west = down(jnp.where(x == 3, nb_we, w[1]), 4)
        from_south = jnp.where(y == 0, up(nb_wn, 3), down(w[3], 1))
        west = self.pack[KEEP_W] * (w[0] - lane_gather(from_west, self.maps[WMAP]))
        south = self.pack[KEEP_S] * (w[2] - lane_gather(from_south, self.maps[SMAP]))
        return west, east, south, north

    def modes(self, r, side):
        return self.pack[M + 4 * r + side]

    def lift(self, row):
        a = jnp.broadcast_to(row, (SUB, LANES))
        pack = self.pack
        w = [0.0] * 4
        t = [0.0] * 2
        nb = [0.0] * 4
        for r in range(MODES):
            own = lane_gather(a, self.own_at(r))
            for side in range(4):
                w[side] += self.modes(r, side) * own
            t[0] += pack[TMW + r] * own
            t[1] += pack[TMS + r] * own
            nb[0] += pack[NB_TMW + r] * lane_gather(a, self.east_at(r))
            nb[1] += pack[NB_ME + r] * lane_gather(a, self.west_at(r))
            nb[2] += pack[NB_TMS + r] * lane_gather(a, self.north_at(r))
            nb[3] += pack[NB_MN + r] * lane_gather(a, self.south_at(r))
        return self.cross(w, t, nb)

    def put(self, total, values, at, rows=None):
        here = self.lane == at
        if rows is not None:
            here = here & rows
        return total + jnp.where(here, jnp.sum(values, axis=1, keepdims=True), 0.0)

    def absorb(self, total, u):
        for r in range(MODES):
            terms = sum(self.modes(r, side) * u[side] for side in range(4))
            total = self.put(total, terms, self.own_at(r))
        return total

    def contributions(self, w, t):
        pack, x, y = self.pack, self.x, self.y
        none = jnp.zeros((SUB, LANES), jnp.float32)
        total = self.absorb(none, self.cross(w, t, (none, none, none, none)))
        to_e, to_w = down(w[1], 4), up(t[0], 4)
        to_n, to_s = up(w[3], 3), down(t[1], 3)
        for r in range(MODES):
            total = self.put(total, -pack[NB_TMW + r] * to_e, self.east_at(r), x == 0)
            total = self.put(total, -pack[NB_ME + r] * to_w, self.west_at(r), x == 3)
            total = self.put(total, -pack[NB_TMS + r] * to_n, self.north_at(r), y == 0)
            total = self.put(total, -pack[NB_MN + r] * to_s, self.south_at(r), y == 3)
        return total

    def dual(self, u, operators, precise):
        whole = jnp.concatenate(u, axis=1)
        left = whole.astype(jnp.bfloat16)
        if precise:
            rest = (whole - left.astype(jnp.float32)).astype(jnp.bfloat16)
            left = jnp.concatenate([left, rest], axis=0)
        row = lax.broadcasted_iota(jnp.int32, (SUB, 4 * E), 0)
        out = jnp.zeros((SUB, 4 * E), jnp.float32)
        for k in range(SUB):
            product = operators.times(k, left)
            if precise:
                product = product[:SUB] + product[SUB:]
            out = jnp.where(row == k, product, out)
        out = operators.finish(out)
        w = [out[:, side * E : (side + 1) * E] for side in range(4)]
        t = lane_gather(w[0], self.maps[WINV]), lane_gather(w[2], self.maps[SINV])
        return w, t

    def send(self, total, edges, ref):
        send_rows(jnp.sum(total, axis=0, keepdims=True), edges, ref)


HALF = 2 * E


class Operators:
    def __init__(self, source, top, low, arrived):
        self.top, self.low = top, low
        self.copies = []
        self.mirrored = jnp.zeros((HALF, LANES), jnp.float32)
        first, rest = pl.ds(0, HALF), pl.ds(HALF, HALF)
        for k in range(SUB):
            whole = source.at[k // 4, k % 4]
            for i, (part, held) in enumerate(((whole.at[first], top), (whole.at[rest, rest], low))):
                copy = pltpu.make_async_copy(part, held.at[k], arrived.at[i, k])
                copy.start()
                self.copies.append(copy)

    def times(self, k, left):
        for copy in self.copies[2 * k : 2 * k + 2]:
            copy.wait()
        first, rest = left[:, :HALF], left[:, HALF:]
        if k == 0:
            filled = jnp.concatenate([rest.astype(jnp.float32), jnp.zeros((LANES - SUB, HALF), jnp.float32)], axis=0)
            self.columns = filled.T.astype(jnp.bfloat16)
        dot = lambda a, b: jnp.dot(a, b, preferred_element_type=jnp.float32)
        beside = self.top[k, :, HALF:]
        lane = lax.broadcasted_iota(jnp.int32, (HALF, LANES), 1)
        self.mirrored = jnp.where(lane == k, dot(beside, self.columns), self.mirrored)
        lower = dot(first, beside) + dot(rest, self.low[k])
        return jnp.concatenate([dot(first, self.top[k, :, :HALF]), lower], axis=1)

    def finish(self, out):
        return jnp.concatenate([out[:, :HALF] + self.mirrored.T[:SUB], out[:, HALF:]], axis=1)


class Held:
    def __init__(self, source):
        self.source = source

    def times(self, k, left):
        return jnp.dot(left, self.source[k // 4, k % 4], preferred_element_type=jnp.float32)

    def finish(self, out):
        return out


EDGE_ROWS = ([0, 1, 2, 3], [12, 13, 14, 15], [0, 4, 8, 12], [3, 7, 11, 15])


def send_rows(row, edges, ref):
    at_x, at_y = lax.axis_index(GX), lax.axis_index(GY)
    no_one = (at_x == 0, at_x == lax.axis_size(GX) - 1, at_y == 0, at_y == lax.axis_size(GY) - 1)
    for half in range(2):
        parts = []
        for arrays, rows, none in zip(edges, EDGE_ROWS, no_one):
            for array in arrays:
                for k in (half, half + 2):
                    parts.append(jnp.where(none, 0.0, array[rows[k] : rows[k] + 1]))
        count = len(parts)
        before, rest = jnp.zeros((AT_EDGE, LANES), jnp.float32), LANES - AT_EDGE - count
        parts = [before, *parts, jnp.zeros((rest, LANES), jnp.float32)]
        turned = jnp.concatenate(parts, axis=0).T
        lane = lax.broadcasted_iota(jnp.int32, (LANES, LANES), 1)
        here = (lane >= AT_EDGE) & (lane < AT_EDGE + count)
        ref[half * LANES : (half + 1) * LANES, :] = jnp.where(here, turned, row)


def arrived_edges(ref, counts):
    halves = [ref[half * LANES : (half + 1) * LANES, :].T for half in range(2)]
    s = lax.broadcasted_iota(jnp.int32, (SUB, LANES), 0)
    at = AT_EDGE
    out = []
    for count, place in zip(counts, (lax.bitwise_and(s, 3),) * 2 + (lax.shift_right_logical(s, 2),) * 2):
        arrays = []
        for _ in range(count):
            rows = [halves[k % 2][at + k // 2 : at + k // 2 + 1] for k in range(4)]
            arrays.append(
                jnp.where(place == 0, rows[0], jnp.where(place == 1, rows[1], jnp.where(place == 2, rows[2], rows[3])))
            )
            at += 2
        out.append(arrays)
    return out


def pass_on(entries, lane, counts):
    ends = []
    at = AT_EDGE
    for count in counts:
        at += 2 * count
        ends.append(at)
    moved = jnp.where(lane < ends[2], up(entries, 1), down(entries, 1))
    return jnp.where(lane < ends[0], up(entries, 8), jnp.where(lane < ends[1], down(entries, 8), moved))


def from_peers(ref):
    return jnp.sum(ref[...], axis=0, keepdims=True)


def scalar(ref, i):
    return ref[0:1, AT_SCALAR + i : AT_SCALAR + i + 1]


def keep(ref, *parts):
    for i, part in enumerate(parts):
        ref[i] = jnp.broadcast_to(part, (SUB, LANES))


LOAD_E, LOAD_N, KEPT_MAPS, KEPT = 20, 21, 22, 26


def start_kernel(loads, owner, west_map, south_map, images, load, out, kept):
    lane = lax.broadcasted_iota(jnp.int32, (E, E), 1)
    at = lax.broadcasted_iota(jnp.int32, (E, E), 0)
    inverses = []
    for source, direct, inverse in ((west_map, WMAP, WINV), (south_map, SMAP, SINV)):
        rows = jnp.concatenate([source[x] for x in range(4)], axis=0)
        kept[KEPT_MAPS + direct] = rows.astype(jnp.float32)
        columns = jnp.concatenate([rows, jnp.zeros((E - SUB, E), jnp.int32)], axis=0).T
        found = []
        for k in range(SUB):
            hit = columns[:, k : k + 1] == lane
            found.append(jnp.sum(jnp.where(hit, at, 0), axis=0, keepdims=True))
        inverses.append(jnp.concatenate(found, axis=0))
        kept[KEPT_MAPS + inverse] = inverses[-1].astype(jnp.float32)
    s = lax.broadcasted_iota(jnp.int32, (SUB, LANES), 0)
    first_x, first_y = lax.axis_index(GX) == 0, lax.axis_index(GY) == 0
    kept[KEEP_W] = jnp.where(first_x & (s < 4), 0.0, 1.0)
    kept[KEEP_S] = jnp.where(first_y & (lax.bitwise_and(s, 3) == 0), 0.0, 1.0)
    for r in range(MODES):
        whole = jnp.concatenate([images[x, r] for x in range(4)], axis=0)
        for side in range(4):
            kept[M + 4 * r + side] = whole[:, side * E : (side + 1) * E]
        kept[TMW + r] = lane_gather(whole[:, :E], inverses[0])
        kept[TMS + r] = lane_gather(whole[:, 2 * E : 3 * E], inverses[1])
    kept[LOAD_E] = jnp.concatenate([load[k // 4, k % 4, 0:1, :] for k in range(SUB)], axis=0)
    kept[LOAD_N] = jnp.concatenate([load[k // 4, k % 4, 1:2, :] for k in range(SUB)], axis=0)

    x = lax.broadcasted_iota(jnp.int32, (8, LANES), 0)
    lane8 = lax.broadcasted_iota(jnp.int32, (8, LANES), 1)
    off = lane8 - 12 * x
    y = sum((off >= c).astype(jnp.int32) for c in (3, 6, 9))
    natural = jnp.zeros((8, LANES), jnp.float32)
    for r in range(MODES):
        block = jnp.concatenate([loads[r], jnp.zeros((4, 4), jnp.float32)], axis=0)
        block = jnp.concatenate([block, jnp.zeros((8, LANES - 4), jnp.float32)], axis=1)
        here = (off >= 0) & (off < 12) & (off - 3 * y == r) & (x < 4)
        natural = natural + jnp.where(here, lane_gather(block, y), 0.0)
    natural = jnp.broadcast_to(jnp.sum(natural, axis=0, keepdims=True), (8, LANES))
    owner_row = jnp.concatenate([owner[...], jnp.zeros((1, LANES - BLOCK), jnp.int32)], axis=1)
    flat = lane_gather(natural, jnp.broadcast_to(owner_row, (8, LANES)))[0:1]
    hit = (jnp.broadcast_to(owner_row, (E, E)).T == lane) & (at < BLOCK)
    inverse = jnp.sum(jnp.where(hit, at, 0), axis=0, keepdims=True).astype(jnp.float32)
    lane1 = lax.broadcasted_iota(jnp.int32, (1, LANES), 1)
    row = jnp.where(lane1 < BLOCK, flat, pltpu.roll(jnp.broadcast_to(inverse, (8, LANES)), BLOCK, 1)[0:1])
    three = lambda first, step: [kept[first + step * r] for r in range(MODES)]
    edges = (
        three(TMW, 1),
        three(M + 1, 4) + [kept[LOAD_E]],
        three(TMS, 1),
        three(M + 3, 4) + [kept[LOAD_N]],
    )
    send_rows(row, edges, out)


def pack_constants(arrived, kept, pack):
    nb_tw, nb_e, nb_ts, nb_n = arrived_edges(arrived, EDGES_SETUP)
    for i in range(LOAD_E):
        pack[i] = kept[i]
    for i in range(4):
        pack[MAPS + i] = kept[KEPT_MAPS + i]
    for r in range(MODES):
        pack[NB_TMW + r] = nb_tw[r]
        pack[NB_ME + r] = nb_e[r]
        pack[NB_TMS + r] = nb_ts[r]
        pack[NB_MN + r] = nb_n[r]
    local = Local(pack)
    none = jnp.zeros((SUB, LANES), jnp.float32)
    load = (none, kept[LOAD_E], none, kept[LOAD_N])
    target = local.cross(load, (none, none), (none, nb_e[MODES], none, nb_n[MODES]))
    for side in range(4):
        pack[TARGET + side] = target[side]
    return local, local.absorb(none, target)


W, T, LAM, G0, COARSE, P1, G1, MOVED = 0, 4, 6, 8, 12, 13, 15, 17


def product_out(local, total, state, w, t, out_row):
    keep(state, *w, *t)
    local.send(total, ([t[0]], [w[1]], [t[1]], [w[3]]), out_row)


def image_of(local, arrived, state):
    w = [state[W + i] for i in range(4)]
    near = [arrays[0] for arrays in arrived_edges(arrived, EDGES)]
    return w, local.cross(w, [state[T], state[T + 1]], near)


def first_kernel(arrived, kept, dual_ops, out_row, state, pack, *rest):
    operators = Operators(dual_ops, *rest)
    local, entries = pack_constants(arrived, kept, pack)
    u = local.lift(from_peers(arrived))
    w, t = local.dual(u, operators, False)
    product_out(local, entries - local.contributions(w, t), state, w, t, out_row)
    state[LAM] = u[1]
    state[LAM + 1] = u[3]


def second_kernel(arrived, pack, dual_ops, before, out_row, state):
    operators = Held(dual_ops)
    local = Local(pack)
    row = from_peers(arrived)
    _, image = image_of(local, arrived, before)
    lifted = local.lift(row)
    g = [pack[TARGET + i] - image[i] - lifted[i] for i in range(4)]
    w, t = local.dual(g, operators, False)
    total = local.contributions(w, t)
    total = local.put(total, g[1] * g[1] + g[3] * g[3], AT_SCALAR)
    total = local.put(total, sum(g[i] * w[i] for i in range(4)), AT_SCALAR + 1)
    product_out(local, total, state, w, t, out_row)
    state[LAM] = before[LAM]
    state[LAM + 1] = before[LAM + 1]
    for i in range(4):
        state[G0 + i] = g[i]
    state[COARSE] = jnp.broadcast_to(row, (SUB, LANES))


def third_kernel(arrived, pack, dual_ops, before, sums, out_row, state):
    operators = Held(dual_ops)
    local = Local(pack)
    alpha = scalar(sums, 0) / scalar(sums, 1)
    row = from_peers(arrived)
    w1, image = image_of(local, arrived, before)
    lifted = local.lift(row)
    p = [image[i] - lifted[i] for i in range(4)]
    g0 = [before[G0 + i] for i in range(4)]
    g = [g0[i] - alpha * p[i] for i in range(4)]
    w, t = local.dual(g, operators, True)
    total = local.contributions(w, t)
    total = local.put(total, g[1] * g[1] + g[3] * g[3], AT_SCALAR)
    total = local.put(total, sum(g[i] * w[i] for i in range(4)), AT_SCALAR + 1)
    total = local.put(total, sum(g0[i] * w[i] + g[i] * w1[i] for i in range(4)), AT_SCALAR + 2)
    product_out(local, total, state, w, t, out_row)
    state[LAM] = before[LAM] + alpha * g0[1]
    state[LAM + 1] = before[LAM + 1] + alpha * g0[3]
    for i in range(4):
        state[G0 + i] = g0[i]
    state[COARSE] = before[COARSE] - alpha * row
    for i, side in ((0, 1), (1, 3)):
        state[P1 + i] = p[side]
        state[G1 + i] = g[side]
    state[MOVED] = jnp.broadcast_to(row, (SUB, LANES))


def last_kernel(arrived, pack, before, sums, sums_next, lam_out, g_out, amplitudes):
    local = Local(pack)
    beta = scalar(sums_next, 0) / scalar(sums, 0)
    curve = scalar(sums_next, 1) + beta * (scalar(sums_next, 2) + beta * scalar(sums, 1))
    alpha = scalar(sums_next, 0) / curve
    row = from_peers(arrived)
    _, image = image_of(local, arrived, before)
    lifted = local.lift(row)
    for i, side in ((0, 1), (1, 3)):
        p = image[side] - lifted[side] + beta * before[P1 + i]
        g_out[:, i, :] = before[G1 + i] - alpha * p
        lam_out[:, i, :] = before[LAM + i] + alpha * (before[G1 + i] + beta * before[G0 + side])
    a = alpha * (row + beta * before[MOVED]) - before[COARSE]
    x = lax.broadcasted_iota(jnp.int32, (SUB, LANES), 0)
    for r in range(MODES):
        at = jnp.minimum(12 * x + 3 * local.lane + r, 127)
        amplitudes[r] = lane_gather(a, at)[:4, :4]


def third_of(lane, base):
    off = lane - base
    return sum((off >= c).astype(jnp.int32) for c in (3, 6, 9)), off


def coarse_body(entries, owner, inverse, factor, out, first=False):
    lane = lax.broadcasted_iota(jnp.int32, (PEERS, LANES), 1)
    group = sum((lane >= c).astype(jnp.int32) for c in (12, 24, 36))
    within = lane - 12 * group
    clip = lambda index: jnp.clip(index, 0, LANES - 1)
    total = entries
    if not first:
        from_e = up(lane_gather(entries, clip(lane + 12)), 8)
        from_w = down(lane_gather(entries, clip(lane + 60)), 8)
        from_n = up(lane_gather(entries, clip(63 + 3 * group + within)), 1)
        from_s = down(lane_gather(entries, clip(84 + 3 * group + within)), 1)
        total = total + jnp.where(lane >= 36, from_e, 0.0) + jnp.where(lane < 12, from_w, 0.0)
        total = total + jnp.where(within >= 9, from_n, 0.0) + jnp.where(within < 3, from_s, 0.0)
    placed = lane_gather(total, owner)
    q = lax.broadcasted_iota(jnp.int32, (8, LANES), 0)
    within = lax.bitwise_and(lax.broadcasted_iota(jnp.int32, (8, LANES), 1) - BLOCK * q, LANES - 1)
    column = jnp.where(within < BLOCK, lax.shift_right_logical(BLOCK * q + within, 7), -1)
    here = [column == j for j in range(3)]
    groups = PEERS // 8
    tile = lambda g, j: factor[:, (3 * g + j) * LANES : (3 * g + j + 1) * LANES]
    y = jnp.zeros((BLOCK, LANES), jnp.float32)
    for g in range(groups):
        rows = placed[8 * g : 8 * g + 8]
        for j in range(3):
            y = y + tile(g, j) * jnp.sum(jnp.where(here[j], rows, 0.0), axis=0, keepdims=True)
    y = jnp.broadcast_to(jnp.sum(y, axis=1, keepdims=True), (BLOCK, LANES))
    spread = []
    for g in range(groups):
        z = [jnp.sum(tile(g, j) * y, axis=0, keepdims=True) for j in range(3)]
        spread.append(jnp.where(here[0], z[0], jnp.where(here[1], z[1], z[2])))
    natural = lane_gather(jnp.concatenate(spread, axis=0), inverse)
    g3, off3 = third_of(lane, AT_S)
    g4, off4 = third_of(lane, AT_N)
    at_w = down(lane_gather(natural, clip(lane - 12)), 8)
    at_e = up(lane_gather(natural, clip(lane - 60)), 8)
    at_s = down(lane_gather(natural, clip(9 * g3 + 9 + off3)), 1)
    at_n = up(lane_gather(natural, clip(9 * g4 + off4)), 1)
    edge = jnp.where(lane < AT_E, at_w, jnp.where(lane < AT_S, at_e, jnp.where(lane < AT_N, at_s, at_n)))
    edges = pass_on(entries, lane, EDGES_SETUP if first else EDGES)
    out[...] = jnp.where(lane < AT_W, natural, jnp.where(lane < AT_EDGE, edge, edges))


def places():
    lane = lax.broadcasted_iota(jnp.int32, (PEERS, LANES), 1)
    return lane, BLOCK * lax.bitwise_and(lax.broadcasted_iota(jnp.int32, (PEERS, LANES), 0), 7)


def coarse_first_kernel(entries, factor, out, inverse_out):
    lane, start = places()
    got = entries[...]
    inverse = jnp.where(lane < BLOCK, pltpu.roll(got, LANES - BLOCK, 1).astype(jnp.int32), lane)
    inverse = lax.bitwise_and(inverse + start, LANES - 1)
    inverse_out[...] = inverse
    coarse_body(got, lax.bitwise_and(lane - start, LANES - 1), inverse, factor, out, True)


def owner_kernel(inverse, owner_out):
    lane, start = places()
    places_of = lax.bitwise_and(inverse[...] - start, LANES - 1)
    owner = lane
    for k in range(BLOCK):
        owner = jnp.where(places_of[:, k : k + 1] == lane, k, owner)
    owner_out[...] = lane_gather(owner, lax.bitwise_and(lane - start, LANES - 1))


def coarse_kernel(entries, owner, inverse, factor, out, *sums):
    got = entries[...]
    for ref in sums:
        ref[...] = jnp.sum(got, axis=0, keepdims=True)
    coarse_body(got, owner[...], inverse[...], factor, out, False)


def f32(*shape):
    return jax.ShapeDtypeStruct(shape, jnp.float32)


def i32(*shape):
    return jax.ShapeDtypeStruct(shape, jnp.int32)


def call(kernel, outs, *args, operators=None, megabytes=16):
    specs = [pl.BlockSpec(memory_space=pltpu.HBM) if i == operators else pl.BlockSpec() for i in range(len(args))]
    scratch = []
    if operators is not None:
        megabytes = 50
        scratch = [
            pltpu.VMEM((SUB, HALF, 4 * E), jnp.bfloat16),
            pltpu.VMEM((SUB, HALF, HALF), jnp.bfloat16),
            pltpu.SemaphoreType.DMA((2, SUB)),
        ]
    return pl.pallas_call(
        kernel,
        out_shape=outs,
        in_specs=specs,
        out_specs=tuple(pl.BlockSpec() for _ in outs),
        scratch_shapes=scratch,
        compiler_params=pltpu.CompilerParams(vmem_limit_bytes=megabytes * 1024 * 1024),
    )(*args)


def settle_kernel(value, inverse, out, owner):
    out[...] = value[...]
    owner_kernel(inverse, owner)


def after(first, *values):
    return lax.optimization_barrier((first, values))


def exchange(rows):
    return lax.all_to_all(rows, ALL, split_axis=0, concat_axis=0, tiled=True)


def shards(dual_ops, dual_load, mode_images, mode_loads, coarse_factor, west_map, south_map, mode_owner):
    rows, row, indices = f32(PEERS, LANES), f32(1, LANES), i32(PEERS, LANES)
    sent, kept = call(
        start_kernel,
        (rows, f32(KEPT, SUB, E)),
        mode_loads.transpose(2, 0, 1),
        mode_owner.reshape(1, BLOCK),
        west_map,
        south_map,
        mode_images.transpose(0, 2, 1, 3),
        dual_load,
        megabytes=60,
    )
    partial, inverse = call(coarse_first_kernel, (rows, indices), exchange(sent), coarse_factor)
    partial, (kept,) = after(partial, kept)
    arrived = exchange(partial)
    kept, owner = call(settle_kernel, (f32(KEPT, SUB, E), indices), kept, inverse)

    def solve(sent, *sums):
        partial, *sums = call(coarse_kernel, (rows, *sums), exchange(sent), owner, inverse, coarse_factor)
        return exchange(partial), *sums

    sent, state, pack = call(
        first_kernel, (rows, f32(8, SUB, E), f32(PACKED, SUB, E)), arrived, kept, dual_ops, operators=2
    )
    (arrived,) = solve(sent)
    sent, state = call(
        second_kernel, (rows, f32(13, SUB, E)), arrived, pack, dual_ops, state
    )
    arrived, sums = solve(sent, row)
    sent, state = call(
        third_kernel, (rows, f32(18, SUB, E)), arrived, pack, dual_ops, state, sums
    )
    arrived, sums_next = solve(sent, row)
    lam, gradient, amplitudes = call(
        last_kernel,
        (f32(SUB, 2, E), f32(SUB, 2, E), f32(MODES, 4, 4)),
        arrived,
        pack,
        state,
        sums,
        sums_next,
    )
    return lam.reshape(4, 4, 2, E), gradient.reshape(4, 4, 2, E), amplitudes.transpose(1, 2, 0)


def solution(mesh):
    placed = (
        P(GX, GY, None, None),
        P(GX, GY, None, None),
        P(GX, GY, None, None),
        P(GX, GY, None),
        P(ALL, None),
        P(GX, GY, None),
        P(GX, GY, None),
        P(ALL),
    )
    return jax.shard_map(
        shards,
        mesh=mesh,
        in_specs=placed,
        out_specs=(P(GX, GY, None, None), P(GX, GY, None, None), P(GX, GY, None)),
        check_vma=False,
    )
```
